32 devices in a mesh: dp: 4 (over z), space: 2 (over x), tensor: 4 (over y, core).
Axes of the slice: x: 2, y: 2, z: 4, core: 2. Of those that a mesh axis runs over, the one named last changes fastest.
Arguments:
- feat_policy: bfloat16 [4, 2, 320, 8, 128], P('dp', None, 'tensor', 'space'), may hold values from -6 to 6
- feat_ref: bfloat16 [4, 2, 320, 8, 128], P('dp', None, 'tensor', 'space'), may hold values from -6 to 6
- noise: float32 [4, 2, 4, 8, 128], P('dp', None, None, 'space'), may hold values from -6 to 6
- w1_policy: bfloat16 [9, 320, 320], P(None, 'tensor'), may hold values from -0.109375 to 0.109375
- w1_ref: bfloat16 [9, 320, 320], P(None, 'tensor'), may hold values from -0.109375 to 0.109375
- b1_policy: float32 [320], P('tensor'), may hold values from -3 to 3
- b1_ref: float32 [320], P('tensor'), may hold values from -3 to 3
- gn_gain_policy: float32 [320], P('tensor'), may hold values from 0.25 to 1.75
- gn_bias_policy: float32 [320], P('tensor'), may hold values from -3 to 3
- gn_gain_ref: float32 [320], P('tensor'), may hold values from 0.25 to 1.75
- gn_bias_ref: float32 [320], P('tensor'), may hold values from -3 to 3
- w2_policy: bfloat16 [9, 4, 320], P(None, None, 'tensor'), may hold values from -0.109375 to 0.109375
- w2_ref: bfloat16 [9, 4, 320], P(None, None, 'tensor'), may hold values from -0.109375 to 0.109375
- time_table: float32 [1000, 320], P(None, 'tensor'), may hold values from -3 to 3
- timestep: int32 [4], P('dp'), may hold values from 0 to 999
- winner: int32 [4], P('dp'), may hold values from 0 to 1
Outputs:
- logits: float32 [4], P('dp')
- grad_w1: float32 [9, 320, 320], P(None, 'tensor', ('dp', 'space'))
- grad_w2: float32 [9, 4, 320], P(None, None, 'tensor')
The draws below stay inside these ranges and needn't reach their ends.
All inputs are finite; a program needn't handle non-finite values.
Results may differ from the reference program's by a relative error of at most 0.0068.
Values may be sent and summed in bfloat16 or wider, within the bound.
A program may use at most 64 MiB of HBM per device.

```python
import jax
import jax.numpy as jnp
from jax import lax

C = 320
OUT_CH = 4
STEPS = 1000
GROUPS = 32
W = 128
H = 8
PAIRS = 4


def place_ends(values, stream_key, smallest, largest):
    longest = values.shape.index(max(values.shape))
    spots = []
    for shift in (0, 1):
        where = [jax.random.randint(jax.random.fold_in(stream_key, axis), (), 0, length) for axis, length in enumerate(values.shape)]
        where[longest] = (where[longest] + shift) % values.shape[longest]
        spots.append(tuple(where))
    return values.at[spots[0]].set(smallest).at[spots[1]].set(largest)


def level_of(key, shape, pieces, smallest, largest):
    def one(dim, blocks):
        heights = jax.random.uniform(jax.random.fold_in(jax.random.fold_in(key, 6), dim), (blocks,), jnp.float32, smallest / len(pieces), largest / len(pieces))
        return jnp.repeat(jnp.exp(heights), shape[dim] // blocks).reshape((-1,) + (1,) * (len(shape) - dim - 1))

    loudness = one(*pieces[0])
    for cut in pieces[1:]:
        loudness = loudness * one(*cut)
    return loudness


def bell_draw(key, shape, scale, limit, shards=(), dtype=jnp.bfloat16):
    factor_of = level_of(key, shape, shards, -0.22, 0.18) if shards else 1.0
    values = jax.random.normal(key, shape, jnp.float32) * scale * factor_of
    return jnp.minimum(jnp.maximum(values, -limit), limit).astype(dtype)


def setup_inputs(seed: int = 0) -> dict:
    streams_of = jax.random.split(jax.random.key(seed), 17)
    feat_policy = bell_draw(streams_of[0], (PAIRS, 2, C, H, W), 1.0, 6.0, ((0, 4), (2, 4), (3, 2)))
    feat_ref = bell_draw(streams_of[1], (PAIRS, 2, C, H, W), 1.0, 6.0, ((0, 4), (2, 4), (3, 2)))
    noise = bell_draw(streams_of[2], (PAIRS, 2, OUT_CH, H, W), 1.0, 6.0, ((0, 4), (3, 2)), jnp.float32)
    w1_policy = bell_draw(streams_of[3], (9, C, C), (9 * C) ** -0.5, 0.109375, ((1, 4),))
    w1_ref = bell_draw(streams_of[4], (9, C, C), (9 * C) ** -0.5, 0.109375, ((1, 4),))
    b1_policy = bell_draw(streams_of[5], (C,), 0.5, 3.0, ((0, 4),), jnp.float32)
    b1_ref = bell_draw(streams_of[6], (C,), 0.5, 3.0, ((0, 4),), jnp.float32)
    gn_gain_policy = jnp.clip(1.0 + 0.15 * jax.random.normal(streams_of[7], (C,), jnp.float32), 0.25, 1.75)
    gn_bias_policy = bell_draw(streams_of[8], (C,), 0.5, 3.0, ((0, 4),), jnp.float32)
    gn_gain_ref = jnp.clip(1.0 + 0.15 * jax.random.normal(streams_of[9], (C,), jnp.float32), 0.25, 1.75)
    gn_bias_ref = bell_draw(streams_of[10], (C,), 0.5, 3.0, ((0, 4),), jnp.float32)
    w2_policy = bell_draw(streams_of[11], (9, OUT_CH, C), (9 * C) ** -0.5, 0.109375, ((2, 4),))
    w2_ref = bell_draw(streams_of[12], (9, OUT_CH, C), (9 * C) ** -0.5, 0.109375, ((2, 4),))
    time_table = bell_draw(streams_of[13], (STEPS, C), 0.5, 3.0, ((1, 4),), jnp.float32)
    timestep = place_ends(jax.random.randint(streams_of[14], (PAIRS,), 0, STEPS), jax.random.fold_in(streams_of[14], 1), 0, STEPS - 1).astype(jnp.int32)
    winner = place_ends(jax.random.randint(streams_of[15], (PAIRS,), 0, 2), jax.random.fold_in(streams_of[15], 1), 0, 1).astype(jnp.int32)
    return dict(feat_policy=feat_policy, feat_ref=feat_ref, noise=noise, w1_policy=w1_policy, w1_ref=w1_ref, b1_policy=b1_policy, b1_ref=b1_ref, gn_gain_policy=gn_gain_policy, gn_bias_policy=gn_bias_policy, gn_gain_ref=gn_gain_ref, gn_bias_ref=gn_bias_ref, w2_policy=w2_policy, w2_ref=w2_ref, time_table=time_table, timestep=timestep, winner=winner)


dpo_beta = 500.0
norm_eps = 1e-05

def to_kernel(weights):
    return weights.reshape(3, 3, weights.shape[1], weights.shape[2]).transpose(2, 3, 0, 1).astype(jnp.float32)

def flip_kernel(weights):
    shaped = weights.reshape(3, 3, weights.shape[1], weights.shape[2])[::-1, ::-1]
    return shaped.transpose(3, 2, 0, 1).astype(jnp.float32)

def conv_same(inputs, kernel):
    return lax.conv_general_dilated(inputs, kernel, (1, 1), ((1, 1), (1, 1)), dimension_numbers=('NCHW', 'OIHW', 'NCHW'), precision=lax.Precision.HIGHEST)

def kernel_grad(inputs, deltas):
    result = lax.conv_general_dilated(inputs, deltas, (1, 1), ((1, 1), (1, 1)), dimension_numbers=('CNHW', 'IOHW', 'NCHW'), precision=lax.Precision.HIGHEST)
    return result.transpose(2, 3, 1, 0).reshape(9, result.shape[1], result.shape[0])

def group_view(values):
    return values.reshape(values.shape[0], GROUPS, C // GROUPS, values.shape[2], values.shape[3])

def group_norm(pre_values, gain_vec, bias_vec):
    shaped = group_view(pre_values)
    group_mean = lax.optimization_barrier(jnp.mean(shaped, axis=(2, 3, 4), keepdims=True))
    group_square = lax.optimization_barrier(jnp.mean(shaped * shaped, axis=(2, 3, 4), keepdims=True))
    inv_std = lax.rsqrt(group_square - group_mean * group_mean + norm_eps)
    centered = ((shaped - group_mean) * inv_std).reshape(pre_values.shape)
    normed = centered * gain_vec[None, :, None, None] + bias_vec[None, :, None, None]
    return (normed, centered, inv_std)

def reference(feat_policy, feat_ref, noise, w1_policy, w1_ref, b1_policy, b1_ref, gn_gain_policy, gn_bias_policy, gn_gain_ref, gn_bias_ref, w2_policy, w2_ref, time_table, timestep, winner):
    kernel_one_policy = to_kernel(w1_policy)
    kernel_one_frozen = to_kernel(w1_ref)
    kernel_two_policy = to_kernel(w2_policy)
    kernel_two_frozen = to_kernel(w2_ref)
    kernel_back = flip_kernel(w2_policy)
    cell_total = OUT_CH * H * W

    def pair_step(carry, inputs):
        grad_one, grad_two = carry
        pair_policy, pair_frozen, pair_noise, step_index, pair_winner = inputs
        shift = time_table[step_index]
        pre_policy = conv_same(pair_policy.astype(jnp.float32), kernel_one_policy) + (b1_policy + shift)[None, :, None, None]
        pre_frozen = conv_same(pair_frozen.astype(jnp.float32), kernel_one_frozen) + (b1_ref + shift)[None, :, None, None]
        normed_policy, centered_policy, inv_policy = group_norm(pre_policy, gn_gain_policy, gn_bias_policy)
        normed_frozen, centered_frozen, inv_frozen = group_norm(pre_frozen, gn_gain_ref, gn_bias_ref)
        hidden_policy = jax.nn.silu(normed_policy).astype(jnp.bfloat16)
        hidden_frozen = jax.nn.silu(normed_frozen).astype(jnp.bfloat16)
        pred_policy = conv_same(hidden_policy.astype(jnp.float32), kernel_two_policy)
        pred_frozen = conv_same(hidden_frozen.astype(jnp.float32), kernel_two_frozen)
        err_policy = lax.optimization_barrier(jnp.mean((pred_policy - pair_noise) ** 2, axis=(1, 2, 3)))
        err_frozen = lax.optimization_barrier(jnp.mean((pred_frozen - pair_noise) ** 2, axis=(1, 2, 3)))
        pair_sign = 1.0 - 2.0 * pair_winner.astype(jnp.float32)
        logit = -0.5 * dpo_beta * pair_sign * (err_policy[0] - err_policy[1] - (err_frozen[0] - err_frozen[1]))
        weight = jax.nn.sigmoid(-logit)
        scaled = dpo_beta * weight * pair_sign / cell_total * jnp.array([1.0, -1.0], jnp.float32)
        dpred = (scaled[:, None, None, None] * (pred_policy - pair_noise)).astype(jnp.bfloat16)
        grad_two = grad_two + kernel_grad(hidden_policy.astype(jnp.float32), dpred.astype(jnp.float32))
        dhidden = conv_same(dpred.astype(jnp.float32), kernel_back)
        gate_value = jax.nn.sigmoid(normed_policy)
        gnorm = dhidden * gate_value * (1.0 + normed_policy * (1.0 - gate_value)) * gn_gain_policy[None, :, None, None]
        grouped_grad = group_view(gnorm)
        grouped_centered = group_view(centered_policy)
        first_mean = lax.optimization_barrier(jnp.mean(grouped_grad, axis=(2, 3, 4), keepdims=True))
        second_mean = lax.optimization_barrier(jnp.mean(grouped_grad * grouped_centered, axis=(2, 3, 4), keepdims=True))
        delta = (inv_policy * (grouped_grad - first_mean - grouped_centered * second_mean)).reshape(pre_policy.shape).astype(jnp.bfloat16)
        grad_one = grad_one + kernel_grad(pair_policy.astype(jnp.float32), delta.astype(jnp.float32))
        return ((grad_one, grad_two), logit)
    start_one = jnp.zeros((9, C, C), jnp.float32)
    start_two = jnp.zeros((9, OUT_CH, C), jnp.float32)
    (grad_one, grad_two), logits = lax.scan(pair_step, (start_one, start_two), (feat_policy, feat_ref, noise, timestep, winner))
    return (logits, grad_one, grad_two)
```

```python
import functools

import jax
import jax.numpy as jnp
from jax import lax
from jax.experimental import pallas as pl
from jax.experimental.pallas import tpu as pltpu
from jax.sharding import PartitionSpec as P

GROUPS = 32
BETA = 500.0
EPS = 1e-05
F32 = jnp.float32
BF16 = jnp.bfloat16
VM = pl.BlockSpec(memory_space=pltpu.VMEM)
SM = pl.BlockSpec(memory_space=pltpu.SMEM)


def flip_bit(index, bit):
    return index + bit - 2 * bit * ((index // bit) % 2)


def dot_nt(a, b):
    return lax.dot_general(a, b, (((1,), (1,)), ((), ())), preferred_element_type=F32)


def shift_right(v, lane):
    return jnp.where(lane == 0, 0.0, pltpu.roll(v, 1, 1))


def shift_left(v, lane):
    cols = v.shape[1]
    return jnp.where(lane == cols - 1, 0.0, pltpu.roll(v, cols - 1, 1))


def kernel(
    dims,
    feat_p, feat_r, noise, w1_p, w1_r, b1_p, b1_r, gain_p, bias_p, gain_r, bias_r,
    w2_p, w2_r, table, timestep, winner,
    logit_out, gw1_out, gw2_out,
    x_buf, pre, hid, stat, pred, res, err, d3, gsend, grecv, w2recv,
    fs, fr, hs, hr, ss, sr, es, er, ps, pr, rs, rr, qs, qr, gs, gr, ws, wr,
):
    n_dp, n_sp, n_t, rows, cols, chan, out_ch = dims
    total = chan * n_t
    parts = n_dp * n_sp
    piece = total // parts
    group = total // GROUPS
    half = rows * cols
    d = lax.axis_index("dp")
    s = lax.axis_index("space")
    t = lax.axis_index("tensor")
    me = d * n_sp + s
    own = pl.ds(pl.multiple_of(t * chan, 16), chan)

    def at(dd=0, ds=0, dt=0):
        return {
            "dp": lax.rem(d + dd, n_dp),
            "space": lax.rem(s + ds + n_sp, n_sp),
            "tensor": lax.rem(t + dt, n_t),
        }

    def remote(src, dst, send, recv, device):
        return pltpu.make_async_remote_copy(
            src_ref=src, dst_ref=dst, send_sem=send, recv_sem=recv,
            device_id=device, device_id_type=pl.DeviceIdType.MESH,
        )

    partners = [(0, ds, dt) for ds in range(n_sp) for dt in range(n_t) if (ds, dt) != (0, 0)]
    partners += [(dd, ds, 0) for dd in range(1, n_dp) for ds in range(n_sp)]
    barrier = pltpu.get_barrier_semaphore()
    for off in partners:
        pl.semaphore_signal(barrier, inc=1, device_id=at(*off), device_id_type=pl.DeviceIdType.MESH)

    ch_i = lax.broadcasted_iota(jnp.int32, (chan, chan * rows), 0)
    ch_j = lax.broadcasted_iota(jnp.int32, (chan, chan * rows), 1)
    order = jnp.concatenate(
        [jnp.where(ch_j == rows * ch_i + y, 1.0, 0.0) for y in range(rows)], axis=0
    ).astype(BF16)
    for m, feat in enumerate((feat_p, feat_r)):
        for i in range(2):
            rowwise = jnp.dot(order, feat[i], preferred_element_type=F32).astype(BF16)
            for y in range(rows):
                x_buf[m, i, 1 + y, own, :] = rowwise[y * chan : (y + 1) * chan]

    @pl.when(s == 0)
    def _():
        x_buf[:, :, 0] = jnp.zeros((2, 2, total, cols), BF16)
        hid[:, :, 0] = jnp.zeros((2, 2, chan, cols), BF16)
        res[0] = jnp.zeros((8, cols), F32)

    @pl.when(s == n_sp - 1)
    def _():
        x_buf[:, :, rows + 1] = jnp.zeros((2, 2, total, cols), BF16)
        hid[:, :, rows + 1] = jnp.zeros((2, 2, chan, cols), BF16)
        res[rows + 1] = jnp.zeros((8, cols), F32)

    stat[...] = jnp.zeros(stat.shape, F32)
    pl.semaphore_wait(barrier, len(partners))

    def halo(down, up):
        def start():
            @pl.when(s < n_sp - 1)
            def _():
                for c in down:
                    c.start()

            @pl.when(s > 0)
            def _():
                for c in up:
                    c.start()

        def arrive():
            @pl.when(s > 0)
            def _():
                for c in down:
                    c.wait_recv()

            @pl.when(s < n_sp - 1)
            def _():
                for c in up:
                    c.wait_recv()

        def finish():
            @pl.when(s < n_sp - 1)
            def _():
                for c in down:
                    c.wait_send()

            @pl.when(s > 0)
            def _():
                for c in up:
                    c.wait_send()

        return start, arrive, finish

    def feat_block(m, i, x):
        low = x & -x
        block = t
        bit = 1
        while bit < n_t:
            if (x ^ low) & bit:
                block = flip_bit(block, bit)
            bit *= 2
        spot = x_buf.at[m, i, pl.ds(1, rows), pl.ds(pl.multiple_of(block * chan, 16), chan), :]
        target = {"dp": d, "space": s, "tensor": flip_bit(t, low)}
        return remote(spot, spot, fs.at[m, i, x - 1], fr.at[m, i, x - 1], target)

    steps = sorted(range(1, n_t), key=lambda x: (bin(x).count("1"), -x))
    blocks = {(m, i, x): feat_block(m, i, x) for m in range(2) for i in range(2) for x in steps}
    feat_halo = []
    for m in range(2):
        down, up = [], []
        for dt in range(n_t):
            for go, ds, a, b, k in ((down, 1, rows, 0, 0), (up, -1, 1, rows + 1, 1)):
                go.append(remote(
                    x_buf.at[m, :, a, own, :], x_buf.at[m, :, b, own, :],
                    hs.at[m, k, dt], hr.at[m, k, dt], at(0, ds, dt),
                ))
        feat_halo.append(halo(down, up))

    for m in range(2):
        for i in range(2):
            for x in steps:
                if x & (x - 1) == 0:
                    blocks[m, i, x].start()
        feat_halo[m][0]()

    def forward(m):
        seen = set()
        for x in steps:
            if x & (x - 1):
                prior = x & (x - 1)
                for i in range(2):
                    if (i, prior) not in seen:
                        blocks[m, i, prior].wait_recv()
                        seen.add((i, prior))
                    blocks[m, i, x].start()
        return seen

    def gathered(m, seen):
        for i in range(2):
            for x in steps:
                if (i, x) not in seen:
                    blocks[m, i, x].wait_recv()
        feat_halo[m][1]()

    ii = lax.broadcasted_iota(jnp.int32, (chan, chan), 0)
    jj = lax.broadcasted_iota(jnp.int32, (chan, chan), 1)
    eye = ii == jj
    same = jnp.zeros((chan, chan), F32)
    for g in range(chan // group):
        lo, hi = g * group, (g + 1) * group
        same += jnp.where((ii >= lo) & (ii < hi) & (jj >= lo) & (jj < hi), 1.0, 0.0)
    lane = lax.broadcasted_iota(jnp.int32, (chan, cols), 1)
    lane8 = lax.broadcasted_iota(jnp.int32, (8, cols), 1)
    lane24 = lax.broadcasted_iota(jnp.int32, (8, cols), 0)

    def column(row):
        return jnp.sum(jnp.where(eye, row, 0.0), axis=1, keepdims=True)

    def group_row(col):
        return jnp.sum(same * col, axis=0, keepdims=True)

    shift = table[pl.ds(timestep[0], 1), :]
    add = [column(b[...] + shift) for b in (b1_p, b1_r)]
    gain = [column(v[...]) for v in (gain_p, gain_r)]
    bias = [column(v[...]) for v in (bias_p, bias_r)]
    count = float(group * rows * n_sp * cols)

    def spread(k):
        copies = [
            remote(stat.at[k, s], stat.at[k, s], ss.at[k, o - 1], sr.at[k, o - 1], at(0, o))
            for o in range(1, n_sp)
        ]
        for c in copies:
            c.start()
        return copies

    def tally(k, lists):
        for i in range(2):
            for j in range(2):
                stat[k, s, 2 * i + j : 2 * i + j + 1, 0:chan] = group_row(lists[i][j])
        return spread(k)

    def collect(k, copies):
        for c in copies:
            c.wait_recv()
        sums = stat[k, 0]
        for o in range(1, n_sp):
            sums = sums + stat[k, o]
        sums = sums * (1.0 / count)
        return [[column(sums[2 * i + j : 2 * i + j + 1, 0:chan]) for j in range(2)] for i in range(2)]

    def first_conv(m):
        w1 = (w1_p, w1_r)[m]
        lists = []
        for i in range(2):
            acc = None
            for ky in range(3):
                cells = jnp.concatenate([x_buf[m, i, ky + y] for y in range(rows)], axis=1)
                taps = w1[3 * ky : 3 * ky + 3].reshape(3 * chan, total)
                term = jnp.dot(taps, cells, preferred_element_type=F32)
                acc = term if acc is None else acc + term
            sums = jnp.zeros((chan, cols), F32)
            squares = jnp.zeros((chan, cols), F32)
            for y in range(rows):
                cut = slice(y * cols, (y + 1) * cols)
                v = acc[chan : 2 * chan, cut] + add[m]
                v = v + shift_right(acc[0:chan, cut], lane)
                v = v + shift_left(acc[2 * chan :, cut], lane)
                pre[m, i, y] = v
                sums = sums + v
                squares = squares + v * v
            lists.append([
                jnp.sum(sums, axis=1, keepdims=True), jnp.sum(squares, axis=1, keepdims=True)
            ])
        return tally(m, lists)

    def edge(buf, send, recv):
        down = [remote(buf(rows), buf(0), send.at[0], recv.at[0], at(0, 1))]
        up = [remote(buf(1), buf(rows + 1), send.at[1], recv.at[1], at(0, -1))]
        return halo(down, up)

    moments = [None, None]

    def activate(m, copies):
        sums = collect(m, copies)
        moments[m] = []
        for i in range(2):
            mean, square = sums[i]
            inv = lax.rsqrt(square - mean * mean + EPS)
            moments[m].append((mean, inv))
            for y in range(rows):
                normed = (pre[m, i, y] - mean) * inv * gain[m] + bias[m]
                hid[m, i, 1 + y] = (normed * jax.nn.sigmoid(normed)).astype(BF16)
        sides = edge(lambda r: hid.at[m, :, r], es.at[m], er.at[m])
        sides[0]()
        return sides

    zero4 = jnp.zeros((8 - out_ch, chan), F32)

    def taps_of(w2):
        first, second = [], []
        for k in range(9):
            w = w2[k].astype(F32)
            first += [w, zero4]
            second += [zero4, w]
        return jnp.concatenate(first, axis=0), jnp.concatenate(second, axis=0)

    taps2 = [taps_of(w2_p), taps_of(w2_r)]

    def second_conv(m, sides):
        sides[1]()
        acc = None
        for i in range(2):
            cells = jnp.concatenate([hid[m, i, r] for r in range(rows + 2)], axis=1)
            term = jnp.dot(taps2[m][i].astype(BF16), cells, preferred_element_type=F32)
            acc = term if acc is None else acc + term
        for y in range(rows):
            by_kx = []
            for kx in range(3):
                v = None
                for ky in range(3):
                    k = 3 * ky + kx
                    term = acc[8 * k : 8 * k + 8, (y + ky) * cols : (y + ky + 1) * cols]
                    v = term if v is None else v + term
                by_kx.append(v)
            pred[m, t, y] = by_kx[1] + shift_right(by_kx[0], lane8) + shift_left(by_kx[2], lane8)
        copies = [
            remote(pred.at[m, t], pred.at[m, t], ps.at[m, o - 1], pr.at[m, o - 1], at(0, 0, o))
            for o in range(1, n_t)
        ]
        for c in copies:
            c.start()
        return copies

    def residual(m, copies):
        for c in copies:
            c.wait_recv()
        squares = jnp.zeros((8, cols), F32)
        for y in range(rows):
            v = pred[m, 0, y]
            for o in range(1, n_t):
                v = v + pred[m, o, y]
            v = v - noise[:, y, :]
            squares = squares + v * v
            if m == 0:
                res[1 + y] = v
        err[m, s] = jnp.broadcast_to(jnp.sum(squares, axis=1, keepdims=True), (8, cols))
        sends = [
            remote(err.at[m, s], err.at[m, s], qs.at[m, o - 1], qr.at[m, o - 1], at(0, o))
            for o in range(1, n_sp)
        ]
        if m == 0:
            sides = edge(lambda r: res.at[r], rs, rr)
            sides[0]()
        for c in sends:
            c.start()
        return (sends, sides) if m == 0 else sends

    pending = []
    seen = forward(0)
    gathered(0, seen)
    stat_p = first_conv(0)
    seen = forward(1)
    side_p = activate(0, stat_p)
    gathered(1, seen)
    stat_r = first_conv(1)
    pred_p = second_conv(0, side_p)
    side_r = activate(1, stat_r)
    err_p, side_d = residual(0, pred_p)
    pred_r = second_conv(1, side_r)

    side_d[1]()
    sign = jnp.where(lane24 < 4, 1.0, -1.0)
    rows3 = []
    for r in range(rows + 2):
        v = res[r] * sign
        v = v.astype(BF16).astype(F32)
        rows3.append(jnp.concatenate([shift_left(v, lane8), v, shift_right(v, lane8)], axis=0))
    spread9 = jnp.concatenate(
        [jnp.concatenate([rows3[y + 2 - ky] for y in range(rows)], axis=1) for ky in range(3)], axis=0
    ).astype(BF16)
    lists = []
    back = []
    for i in range(2):
        mean, inv = moments[0][i]
        flipped = jnp.transpose(taps2[0][i]).astype(BF16)
        dh = jnp.dot(flipped, spread9, preferred_element_type=F32)
        first = jnp.zeros((chan, cols), F32)
        second = jnp.zeros((chan, cols), F32)
        keep = []
        for y in range(rows):
            xhat = (pre[0, i, y] - mean) * inv
            normed = xhat * gain[0] + bias[0]
            gate = jax.nn.sigmoid(normed)
            g = dh[:, y * cols : (y + 1) * cols] * gate * (1.0 + normed * (1.0 - gate)) * gain[0]
            first = first + g
            second = second + g * xhat
            pre[0, i, y] = xhat
            pre[1, i, y] = g
        lists.append([jnp.sum(first, axis=1, keepdims=True), jnp.sum(second, axis=1, keepdims=True)])
    stat_b = tally(2, lists)

    center = jnp.concatenate(rows3[1 : rows + 1], axis=1)
    half_row = lax.broadcasted_iota(jnp.int32, center.shape, 0)
    in_first = (half_row % 8) < 4
    w2_sum = [None] * 3
    for i in range(2):
        mine = jnp.where(in_first if i == 0 else jnp.logical_not(in_first), center, 0.0).astype(BF16)
        for ky in range(3):
            cells = jnp.concatenate([hid[0, i, ky + y] for y in range(rows)], axis=1)
            term = dot_nt(mine, cells)
            w2_sum[ky] = term if w2_sum[ky] is None else w2_sum[ky] + term

    err_r = residual(1, pred_r)
    sums = collect(2, stat_b)
    for i in range(2):
        a, b = sums[i]
        inv = moments[0][i][1]
        for y in range(rows):
            v = inv * (pre[1, i, y] - a - pre[0, i, y] * b)
            cut = slice(y * cols, (y + 1) * cols)
            d3[i, 0:chan, cut] = shift_left(v, lane).astype(BF16)
            d3[i, chan : 2 * chan, cut] = v.astype(BF16)
            d3[i, 2 * chan : 3 * chan, cut] = shift_right(v, lane).astype(BF16)

    for c in err_p + err_r:
        c.wait_recv()
    gaps = []
    for m in range(2):
        v = err[m, 0]
        for o in range(1, n_sp):
            v = v + err[m, o]
        v = v * (1.0 / (out_ch * half * n_sp))
        gaps.append(jnp.sum(v * sign, axis=0, keepdims=True))
    pair_sign = 1.0 - 2.0 * winner[0].astype(F32)
    logit = (-0.5 * BETA) * pair_sign * (gaps[0] - gaps[1])
    logit_out[...] = logit
    factor = (BETA / (out_ch * half * n_sp)) * pair_sign * jax.nn.sigmoid(-logit)[:, 0:1]

    others = [(dd, ds) for dd in range(n_dp) for ds in range(n_sp) if (dd, ds) != (0, 0)]
    others.sort(key=lambda o: -min(o[0], n_dp - o[0]))
    taps = [w2_sum[k // 3][8 * (k % 3) : 8 * (k % 3) + 8] for k in range(9)]
    taps = [(v + pltpu.roll(v, 4, 0)) * factor for v in taps] + [jnp.zeros((8, chan), F32)]
    upper = lax.broadcasted_iota(jnp.int32, (8, chan), 0) < 4
    for j in range(5):
        w2recv[me, 8 * j : 8 * j + 8] = jnp.where(upper, taps[2 * j], taps[2 * j + 1])
    w2_sends = [
        remote(w2recv.at[me], w2recv.at[me], ws.at[dd * n_sp + ds], wr.at[dd * n_sp + ds], at(dd, ds))
        for dd, ds in others
    ]
    for c in w2_sends:
        c.start()

    grads = []
    for ky in range(3):
        acc = None
        for i in range(2):
            cells = jnp.concatenate([x_buf[0, i, ky + y] for y in range(rows)], axis=1)
            term = dot_nt(cells, d3[i])
            acc = term if acc is None else acc + term
        grads.append(acc * factor)
    spare = gsend.shape[1] - 3 * piece
    for p in range(parts):
        block = [g[p * piece : (p + 1) * piece] for g in grads]
        if spare:
            block.append(jnp.zeros((spare, 3 * chan), F32))
        gsend[p] = jnp.concatenate(block, axis=0).astype(BF16)
    g_sends = []
    for dd, ds in others:
        target = lax.rem(d + dd, n_dp) * n_sp + lax.rem(s + ds, n_sp)
        k = dd * n_sp + ds
        g_sends.append(remote(gsend.at[target], grecv.at[me], gs.at[k], gr.at[k], at(dd, ds)))
    for c in g_sends:
        c.start()
    grecv[me] = gsend[me]

    for c in w2_sends:
        c.wait_recv()
    v = w2recv[0]
    for o in range(1, parts):
        v = v + w2recv[o]
    for k in range(9):
        gw2_out[k] = v[4 * k : 4 * k + 4]

    for c in g_sends:
        c.wait_recv()
    v = grecv[0].astype(F32)
    for o in range(1, parts):
        v = v + grecv[o].astype(F32)
    for ky in range(3):
        turned = jnp.transpose(v[ky * piece : (ky + 1) * piece])
        for kx in range(3):
            gw1_out[3 * ky + kx] = turned[kx * chan : (kx + 1) * chan]

    for c in blocks.values():
        c.wait_send()
    for sides in (feat_halo[0], feat_halo[1], side_p, side_r, side_d):
        sides[2]()
    for c in stat_p + stat_r + stat_b + pred_p + pred_r + err_p + err_r + w2_sends + g_sends:
        c.wait_send()


def body(
    feat_policy, feat_ref, noise, w1_policy, w1_ref, b1_policy, b1_ref,
    gn_gain_policy, gn_bias_policy, gn_gain_ref, gn_bias_ref,
    w2_policy, w2_ref, time_table, timestep, winner,
):
    _, latents, chan, rows, cols = feat_policy.shape
    out_ch = noise.shape[2]
    n_dp, n_sp, n_t = (lax.axis_size(a) for a in ("dp", "space", "tensor"))
    total, parts = chan * n_t, n_dp * n_sp
    piece = total // parts
    deep = -(-3 * piece // 16) * 16
    dma = pltpu.SemaphoreType.DMA
    near, far = max(n_sp - 1, 1), max(n_t - 1, 1)
    scratch = [
        pltpu.VMEM((2, 2, rows + 2, total, cols), BF16),
        pltpu.VMEM((2, 2, rows, chan, cols), F32),
        pltpu.VMEM((2, 2, rows + 2, chan, cols), BF16),
        pltpu.VMEM((3, n_sp, 8, cols), F32),
        pltpu.VMEM((2, n_t, rows, 8, cols), F32),
        pltpu.VMEM((rows + 2, 8, cols), F32),
        pltpu.VMEM((2, n_sp, 8, cols), F32),
        pltpu.VMEM((2, 3 * chan, rows * cols), BF16),
        pltpu.VMEM((parts, deep, 3 * chan), BF16),
        pltpu.VMEM((parts, deep, 3 * chan), BF16),
        pltpu.VMEM((parts, 40, chan), F32),
    ]
    for shape in (
        (2, 2, far), (2, 2, n_t), (3, near), (2, 2), (2, far), (2,), (2, near), (parts,), (parts,)
    ):
        scratch += [dma(shape), dma(shape)]
    dims = (n_dp, n_sp, n_t, rows, cols, chan, out_ch)
    logit, gw1, gw2 = pl.pallas_call(
        functools.partial(kernel, dims),
        out_shape=[
            jax.ShapeDtypeStruct((1, cols), F32),
            jax.ShapeDtypeStruct((9, chan, piece), F32),
            jax.ShapeDtypeStruct((9, out_ch, chan), F32),
        ],
        in_specs=[VM] * 14 + [SM] * 2,
        out_specs=[VM] * 3,
        scratch_shapes=scratch,
        compiler_params=pltpu.CompilerParams(
            collective_id=0, has_side_effects=True, vmem_limit_bytes=40 * 1024 * 1024
        ),
        name="dpo",
    )(
        feat_policy.reshape(latents, chan * rows, cols),
        feat_ref.reshape(latents, chan * rows, cols),
        noise.reshape(latents * out_ch, rows, cols),
        w1_policy, w1_ref,
        b1_policy[None], b1_ref[None],
        gn_gain_policy[None], gn_bias_policy[None], gn_gain_ref[None], gn_bias_ref[None],
        w2_policy, w2_ref, time_table, timestep, winner,
    )
    return logit[0, :1], gw1, gw2


def solution(mesh):
    in_specs = (
        P("dp", None, "tensor", "space", None),
        P("dp", None, "tensor", "space", None),
        P("dp", None, None, "space", None),
        P(None, "tensor", None),
        P(None, "tensor", None),
        P("tensor"),
        P("tensor"),
        P("tensor"),
        P("tensor"),
        P("tensor"),
        P("tensor"),
        P(None, None, "tensor"),
        P(None, None, "tensor"),
        P(None, "tensor"),
        P("dp"),
        P("dp"),
    )
    out_specs = (P("dp"), P(None, "tensor", ("dp", "space")), P(None, None, "tensor"))
    return jax.shard_map(body, mesh=mesh, in_specs=in_specs, out_specs=out_specs, check_vma=False)
```

```python
import functools

import jax
import jax.numpy as jnp
from jax import lax
from jax.experimental import pallas as pl
from jax.experimental.pallas import tpu as pltpu
from jax.sharding import PartitionSpec as P

GROUPS = 32
BETA = 500.0
EPS = 1e-05
F32 = jnp.float32
BF16 = jnp.bfloat16
VM = pl.BlockSpec(memory_space=pltpu.VMEM)
SM = pl.BlockSpec(memory_space=pltpu.SMEM)


def flip_bit(index, bit):
    return index + bit - 2 * bit * ((index // bit) % 2)


def dot_nt(a, b):
    return lax.dot_general(a, b, (((1,), (1,)), ((), ())), preferred_element_type=F32)


def shift_right(v, lane):
    return jnp.where(lane == 0, 0.0, pltpu.roll(v, 1, 1))


def shift_left(v, lane):
    cols = v.shape[1]
    return jnp.where(lane == cols - 1, 0.0, pltpu.roll(v, cols - 1, 1))


def kernel(
    dims,
    *refs,
):
    far_in, (timestep, winner, logit_out, gw1_out, gw2_out) = refs[:14], refs[14:19]
    near_in, load_sem = refs[19:33], refs[33]
    (
        x_buf, w1_all, pre, hid, stat, pred, res, err, d3, gsend, grecv, zsend, zrecv, w2x, w2z,
        fs, fr, hs, hr, ss, sr, es, er, ps, pr, rs, rr, qs, qr, gs, gr, zs, zr, ws, wr, vs, vr,
    ) = refs[34:]
    (
        feat_p, feat_r, noise, w1_p, w1_r, b1_p, b1_r, gain_p, bias_p, gain_r, bias_r,
        w2_p, w2_r, table,
    ) = near_in
    loads = [
        pltpu.make_async_copy(a, b, load_sem.at[k])
        for k, (a, b) in enumerate(zip(far_in, near_in))
    ]
    for c in loads:
        c.start()
    n_dp, n_sp, n_t, rows, cols, chan, out_ch = dims
    total = chan * n_t
    parts = n_dp * n_sp
    piece = total // parts
    group = total // GROUPS
    half = rows * cols
    d = lax.axis_index("dp")
    s = lax.axis_index("space")
    t = lax.axis_index("tensor")
    me = d * n_sp + s
    own = pl.ds(pl.multiple_of(t * chan, 16), chan)

    def at(dd=0, ds=0, dt=0):
        return {
            "dp": lax.rem(d + dd, n_dp),
            "space": lax.rem(s + ds + n_sp, n_sp),
            "tensor": lax.rem(t + dt, n_t),
        }

    def remote(src, dst, send, recv, device):
        return pltpu.make_async_remote_copy(
            src_ref=src, dst_ref=dst, send_sem=send, recv_sem=recv,
            device_id=device, device_id_type=pl.DeviceIdType.MESH,
        )

    partners = [(0, ds, dt) for ds in range(n_sp) for dt in range(n_t) if (ds, dt) != (0, 0)]
    partners += [(dd, 0, 0) for dd in range(1, n_dp)]
    barrier = pltpu.get_barrier_semaphore()
    for off in partners:
        pl.semaphore_signal(barrier, inc=1, device_id=at(*off), device_id_type=pl.DeviceIdType.MESH)

    ch_i = lax.broadcasted_iota(jnp.int32, (chan, chan * rows), 0)
    ch_j = lax.broadcasted_iota(jnp.int32, (chan, chan * rows), 1)
    order = jnp.concatenate(
        [jnp.where(ch_j == rows * ch_i + y, 1.0, 0.0) for y in range(rows)], axis=0
    ).astype(BF16)
    for m, feat in enumerate((feat_p, feat_r)):
        loads[m].wait()
        for i in range(2):
            rowwise = jnp.dot(order, feat[i], preferred_element_type=F32).astype(BF16)
            for y in range(rows):
                x_buf[m, i, 1 + y, own, :] = rowwise[y * chan : (y + 1) * chan]

    @pl.when(s == 0)
    def _():
        x_buf[:, :, 0] = jnp.zeros((2, 2, total, cols), BF16)
        hid[:, :, 0] = jnp.zeros((2, 2, chan, cols), BF16)
        res[0] = jnp.zeros((8, cols), F32)

    @pl.when(s == n_sp - 1)
    def _():
        x_buf[:, :, rows + 1] = jnp.zeros((2, 2, total, cols), BF16)
        hid[:, :, rows + 1] = jnp.zeros((2, 2, chan, cols), BF16)
        res[rows + 1] = jnp.zeros((8, cols), F32)

    stat[...] = jnp.zeros(stat.shape, F32)
    pl.semaphore_wait(barrier, len(partners))

    def halo(down, up):
        def start():
            @pl.when(s < n_sp - 1)
            def _():
                for c in down:
                    c.start()

            @pl.when(s > 0)
            def _():
                for c in up:
                    c.start()

        def arrive():
            @pl.when(s > 0)
            def _():
                for c in down:
                    c.wait_recv()

            @pl.when(s < n_sp - 1)
            def _():
                for c in up:
                    c.wait_recv()

        def finish():
            @pl.when(s < n_sp - 1)
            def _():
                for c in down:
                    c.wait_send()

            @pl.when(s > 0)
            def _():
                for c in up:
                    c.wait_send()

        return start, arrive, finish

    def feat_block(m, i, x):
        low = x & -x
        block = t
        bit = 1
        while bit < n_t:
            if (x ^ low) & bit:
                block = flip_bit(block, bit)
            bit *= 2
        spot = x_buf.at[m, i, pl.ds(1, rows), pl.ds(pl.multiple_of(block * chan, 16), chan), :]
        target = {"dp": d, "space": s, "tensor": flip_bit(t, low)}
        return remote(spot, spot, fs.at[m, i, x - 1], fr.at[m, i, x - 1], target)

    steps = sorted(range(1, n_t), key=lambda x: (bin(x).count("1"), -x))
    blocks = {(m, i, x): feat_block(m, i, x) for m in range(2) for i in range(2) for x in steps}
    feat_halo = []
    for m in range(2):
        down, up = [], []
        for dt in range(n_t):
            for go, ds, a, b, k in ((down, 1, rows, 0, 0), (up, -1, 1, rows + 1, 1)):
                go.append(remote(
                    x_buf.at[m, :, a, own, :], x_buf.at[m, :, b, own, :],
                    hs.at[m, k, dt], hr.at[m, k, dt], at(0, ds, dt),
                ))
        feat_halo.append(halo(down, up))

    def send_features(m):
        for i in range(2):
            for x in steps:
                if x & (x - 1) == 0:
                    blocks[m, i, x].start()
        feat_halo[m][0]()

    send_features(0)

    def forward(m):
        seen = set()
        for x in steps:
            if x & (x - 1):
                prior = x & (x - 1)
                for i in range(2):
                    if (i, prior) not in seen:
                        blocks[m, i, prior].wait_recv()
                        seen.add((i, prior))
                    blocks[m, i, x].start()
        return seen

    def gathered(m, i, seen):
        for x in steps:
            if (i, x) not in seen:
                blocks[m, i, x].wait_recv()
        if i == 0:
            feat_halo[m][1]()

    for c in loads[2:]:
        c.wait()
    for m, w1 in enumerate((w1_p, w1_r)):
        w1_all[m] = jnp.concatenate(
            [w1[3 * ky : 3 * ky + 3].reshape(3 * chan, total) for ky in range(3)], axis=1
        )

    ii = lax.broadcasted_iota(jnp.int32, (chan, chan), 0)
    jj = lax.broadcasted_iota(jnp.int32, (chan, chan), 1)
    eye = ii == jj
    same = jnp.zeros((chan, chan), F32)
    for g in range(chan // group):
        lo, hi = g * group, (g + 1) * group
        same += jnp.where((ii >= lo) & (ii < hi) & (jj >= lo) & (jj < hi), 1.0, 0.0)
    lane = lax.broadcasted_iota(jnp.int32, (chan, cols), 1)
    lane8 = lax.broadcasted_iota(jnp.int32, (8, cols), 1)
    lane24 = lax.broadcasted_iota(jnp.int32, (8, cols), 0)

    def column(row):
        return jnp.sum(jnp.where(eye, row, 0.0), axis=1, keepdims=True)

    def group_row(col):
        return jnp.sum(same * col, axis=0, keepdims=True)

    step_i = lax.broadcasted_iota(jnp.int32, table.shape, 1)
    shift = jnp.sum(jnp.where(step_i == timestep[0], table[...], 0.0), axis=1, keepdims=True)
    add = [column(b[...]) + shift for b in (b1_p, b1_r)]
    gain = [column(v[...]) for v in (gain_p, gain_r)]
    bias = [column(v[...]) for v in (bias_p, bias_r)]
    count = float(group * rows * n_sp * cols)

    def spread(k):
        copies = [
            remote(stat.at[k, s], stat.at[k, s], ss.at[k, o - 1], sr.at[k, o - 1], at(0, o))
            for o in range(1, n_sp)
        ]
        for c in copies:
            c.start()
        return copies

    def tally(k, lists):
        for i in range(2):
            for j in range(2):
                stat[k, s, 2 * i + j : 2 * i + j + 1, 0:chan] = group_row(lists[i][j])
        return spread(k)

    def collect(k, copies):
        for c in copies:
            c.wait_recv()
        sums = stat[k, 0]
        for o in range(1, n_sp):
            sums = sums + stat[k, o]
        sums = sums * (1.0 / count)
        return [[column(sums[2 * i + j : 2 * i + j + 1, 0:chan]) for j in range(2)] for i in range(2)]

    def window(m, i):
        return jnp.concatenate(
            [
                jnp.concatenate([x_buf[m, i, ky + y] for y in range(rows)], axis=1)
                for ky in range(3)
            ],
            axis=0,
        )

    def first_conv(m, seen):
        lists = []
        for i in range(2):
            gathered(m, i, seen)
            acc = jnp.dot(w1_all[m], window(m, i), preferred_element_type=F32)
            sums = jnp.zeros((chan, cols), F32)
            squares = jnp.zeros((chan, cols), F32)
            for y in range(rows):
                cut = slice(y * cols, (y + 1) * cols)
                v = acc[chan : 2 * chan, cut] + add[m]
                v = v + shift_right(acc[0:chan, cut], lane)
                v = v + shift_left(acc[2 * chan :, cut], lane)
                pre[m, i, y] = v
                sums = sums + v
                squares = squares + v * v
            lists.append([
                jnp.sum(sums, axis=1, keepdims=True), jnp.sum(squares, axis=1, keepdims=True)
            ])
        return tally(m, lists)

    def edge(buf, send, recv):
        down = [remote(buf(rows), buf(0), send.at[0], recv.at[0], at(0, 1))]
        up = [remote(buf(1), buf(rows + 1), send.at[1], recv.at[1], at(0, -1))]
        return halo(down, up)

    moments = [None, None]

    def activate(m, copies):
        sums = collect(m, copies)
        moments[m] = []
        for i in range(2):
            mean, square = sums[i]
            inv = lax.rsqrt(square - mean * mean + EPS)
            moments[m].append((mean, inv))
            for y in range(rows):
                normed = (pre[m, i, y] - mean) * inv * gain[m] + bias[m]
                hid[m, i, 1 + y] = (normed * jax.nn.sigmoid(normed)).astype(BF16)
        sides = edge(lambda r: hid.at[m, :, r], es.at[m], er.at[m])
        sides[0]()
        return sides

    zero4 = jnp.zeros((8 - out_ch, chan), F32)

    def taps_of(w2):
        first, second = [], []
        for k in range(9):
            w = w2[k].astype(F32)
            first += [w, zero4]
            second += [zero4, w]
        return jnp.concatenate(first, axis=0), jnp.concatenate(second, axis=0)

    taps2 = [taps_of(w2_p), taps_of(w2_r)]

    def second_conv(m, sides):
        sides[1]()
        acc = None
        for i in range(2):
            cells = jnp.concatenate([hid[m, i, r] for r in range(rows + 2)], axis=1)
            term = jnp.dot(taps2[m][i].astype(BF16), cells, preferred_element_type=F32)
            acc = term if acc is None else acc + term
        for y in range(rows):
            by_kx = []
            for kx in range(3):
                v = None
                for ky in range(3):
                    k = 3 * ky + kx
                    term = acc[8 * k : 8 * k + 8, (y + ky) * cols : (y + ky + 1) * cols]
                    v = term if v is None else v + term
                by_kx.append(v)
            pred[m, t, y] = by_kx[1] + shift_right(by_kx[0], lane8) + shift_left(by_kx[2], lane8)
        copies = [
            remote(pred.at[m, t], pred.at[m, t], ps.at[m, o - 1], pr.at[m, o - 1], at(0, 0, o))
            for o in range(1, n_t)
        ]
        for c in copies:
            c.start()
        return copies

    def residual(m, copies):
        for c in copies:
            c.wait_recv()
        squares = jnp.zeros((8, cols), F32)
        for y in range(rows):
            v = pred[m, 0, y]
            for o in range(1, n_t):
                v = v + pred[m, o, y]
            v = v - noise[:, y, :]
            squares = squares + v * v
            if m == 0:
                res[1 + y] = v
        err[m, s] = jnp.broadcast_to(jnp.sum(squares, axis=1, keepdims=True), (8, cols))
        sends = [
            remote(err.at[m, s], err.at[m, s], qs.at[m, o - 1], qr.at[m, o - 1], at(0, o))
            for o in range(1, n_sp)
        ]
        if m == 0:
            sides = edge(lambda r: res.at[r], rs, rr)
            sides[0]()
        for c in sends:
            c.start()
        return (sends, sides) if m == 0 else sends

    pending = []
    seen = forward(0)
    send_features(1)
    stat_p = first_conv(0, seen)
    side_p = activate(0, stat_p)
    seen = forward(1)
    stat_r = first_conv(1, seen)
    pred_p = second_conv(0, side_p)
    side_r = activate(1, stat_r)
    err_p, side_d = residual(0, pred_p)
    pred_r = second_conv(1, side_r)

    side_d[1]()
    sign = jnp.where(lane24 < 4, 1.0, -1.0)
    rows3 = []
    for r in range(rows + 2):
        v = res[r] * sign
        v = v.astype(BF16).astype(F32)
        rows3.append(jnp.concatenate([shift_left(v, lane8), v, shift_right(v, lane8)], axis=0))
    spread9 = jnp.concatenate(
        [jnp.concatenate([rows3[y + 2 - ky] for y in range(rows)], axis=1) for ky in range(3)], axis=0
    ).astype(BF16)
    lists = []
    back = []
    for i in range(2):
        mean, inv = moments[0][i]
        flipped = jnp.transpose(taps2[0][i]).astype(BF16)
        dh = jnp.dot(flipped, spread9, preferred_element_type=F32)
        first = jnp.zeros((chan, cols), F32)
        second = jnp.zeros((chan, cols), F32)
        keep = []
        for y in range(rows):
            xhat = (pre[0, i, y] - mean) * inv
            normed = xhat * gain[0] + bias[0]
            gate = jax.nn.sigmoid(normed)
            g = dh[:, y * cols : (y + 1) * cols] * gate * (1.0 + normed * (1.0 - gate)) * gain[0]
            first = first + g
            second = second + g * xhat
            pre[0, i, y] = xhat
            pre[1, i, y] = g
        lists.append([jnp.sum(first, axis=1, keepdims=True), jnp.sum(second, axis=1, keepdims=True)])
    stat_b = tally(2, lists)

    center = jnp.concatenate(rows3[1 : rows + 1], axis=1)
    half_row = lax.broadcasted_iota(jnp.int32, center.shape, 0)
    in_first = (half_row % 8) < 4
    w2_sum = [None] * 3
    for i in range(2):
        mine = jnp.where(in_first if i == 0 else jnp.logical_not(in_first), center, 0.0).astype(BF16)
        for ky in range(3):
            cells = jnp.concatenate([hid[0, i, ky + y] for y in range(rows)], axis=1)
            term = dot_nt(mine, cells)
            w2_sum[ky] = term if w2_sum[ky] is None else w2_sum[ky] + term

    taps = [w2_sum[k // 3][8 * (k % 3) : 8 * (k % 3) + 8] for k in range(9)]
    taps = [v + pltpu.roll(v, 4, 0) for v in taps] + [jnp.zeros((8, chan), F32)]
    upper = lax.broadcasted_iota(jnp.int32, (8, chan), 0) < 4
    for j in range(5):
        w2x[s, 8 * j : 8 * j + 8] = jnp.where(upper, taps[2 * j], taps[2 * j + 1])
    w2_near = [
        remote(w2x.at[s], w2x.at[s], ws.at[o - 1], wr.at[o - 1], at(0, o)) for o in range(1, n_sp)
    ]
    for c in w2_near:
        c.start()

    err_r = residual(1, pred_r)
    sums = collect(2, stat_b)
    for i in range(2):
        a, b = sums[i]
        inv = moments[0][i][1]
        for y in range(rows):
            v = inv * (pre[1, i, y] - a - pre[0, i, y] * b)
            cut = slice((i * rows + y) * cols, (i * rows + y + 1) * cols)
            d3[0:chan, cut] = shift_left(v, lane).astype(BF16)
            d3[chan : 2 * chan, cut] = v.astype(BF16)
            d3[2 * chan : 3 * chan, cut] = shift_right(v, lane).astype(BF16)

    cells = jnp.concatenate([window(0, i) for i in range(2)], axis=1)
    grads = dot_nt(cells, d3[...])
    spare = gsend.shape[1] - 3 * piece
    for p in range(parts):
        block = [grads[ky * total + p * piece : ky * total + (p + 1) * piece] for ky in range(3)]
        if spare:
            block.append(jnp.zeros((spare, 3 * chan), F32))
        gsend[p] = jnp.concatenate(block, axis=0).astype(BF16)
    order_dp = sorted(range(1, n_dp), key=lambda o: -min(o, n_dp - o)) + [0]
    g_near = {}
    for dd in order_dp:
        there = lax.rem(d + dd, n_dp)
        for o in range(1, n_sp):
            target = there * n_sp + lax.rem(s + o, n_sp)
            c = remote(
                gsend.at[target], grecv.at[there, s], gs.at[dd, o - 1], gr.at[dd, o - 1], at(0, o)
            )
            c.start()
            g_near[dd, o] = c

    for c in err_p + err_r:
        c.wait_recv()
    gaps = []
    for m in range(2):
        v = err[m, 0]
        for o in range(1, n_sp):
            v = v + err[m, o]
        v = v * (1.0 / (out_ch * half * n_sp))
        gaps.append(jnp.sum(v * sign, axis=0, keepdims=True))
    pair_sign = 1.0 - 2.0 * winner[0].astype(F32)
    logit = (-0.5 * BETA) * pair_sign * (gaps[0] - gaps[1])
    logit_out[...] = logit
    factor = (BETA / (out_ch * half * n_sp)) * pair_sign * jax.nn.sigmoid(-logit)[:, 0:1]

    for c in w2_near:
        c.wait_recv()
    v = w2x[0]
    for o in range(1, n_sp):
        v = v + w2x[o]
    w2z[d] = v * factor
    w2_far = [
        remote(w2z.at[d], w2z.at[d], vs.at[dd - 1], vr.at[dd - 1], at(dd)) for dd in range(1, n_dp)
    ]
    for c in w2_far:
        c.start()

    g_far = []
    mine = None
    for dd in order_dp:
        there = lax.rem(d + dd, n_dp)
        v = gsend[there * n_sp + s].astype(F32)
        for o in range(1, n_sp):
            g_near[dd, o].wait_recv()
            v = v + grecv[there, lax.rem(s + n_sp - o, n_sp)].astype(F32)
        v = v * factor
        if dd == 0:
            mine = v
        else:
            zsend[there] = v.astype(BF16)
            c = remote(zsend.at[there], zrecv.at[d], zs.at[dd - 1], zr.at[dd - 1], at(dd))
            c.start()
            g_far.append(c)

    for c in w2_far:
        c.wait_recv()
    v = w2z[0]
    for o in range(1, n_dp):
        v = v + w2z[o]
    for k in range(9):
        gw2_out[k] = v[4 * k : 4 * k + 4]

    for c in g_far:
        c.wait_recv()
    for dd in range(1, n_dp):
        mine = mine + zrecv[lax.rem(d + dd, n_dp)].astype(F32)
    for ky in range(3):
        for kx in range(3):
            gw1_out[3 * ky + kx] = mine[ky * piece : (ky + 1) * piece, kx * chan : (kx + 1) * chan]

    for c in blocks.values():
        c.wait_send()
    for sides in (feat_halo[0], feat_halo[1], side_p, side_r, side_d):
        sides[2]()
    for c in stat_p + stat_r + stat_b + pred_p + pred_r + err_p + err_r + w2_near + w2_far + g_far:
        c.wait_send()
    for c in g_near.values():
        c.wait_send()


def body(
    feat_policy, feat_ref, noise, w1_policy, w1_ref, b1_policy, b1_ref,
    gn_gain_policy, gn_bias_policy, gn_gain_ref, gn_bias_ref,
    w2_policy, w2_ref, time_table, timestep, winner,
):
    _, latents, chan, rows, cols = feat_policy.shape
    out_ch = noise.shape[2]
    n_dp, n_sp, n_t = (lax.axis_size(a) for a in ("dp", "space", "tensor"))
    total, parts = chan * n_t, n_dp * n_sp
    piece = total // parts
    deep = -(-3 * piece // 16) * 16
    dma = pltpu.SemaphoreType.DMA
    near, far = max(n_sp - 1, 1), max(n_t - 1, 1)
    operands = [
        feat_policy.reshape(latents, chan * rows, cols),
        feat_ref.reshape(latents, chan * rows, cols),
        noise.reshape(latents * out_ch, rows, cols),
        w1_policy, w1_ref,
        b1_policy[None], b1_ref[None],
        gn_gain_policy[None], gn_bias_policy[None], gn_gain_ref[None], gn_bias_ref[None],
        w2_policy, w2_ref, time_table.T,
    ]
    scratch = [pltpu.VMEM(a.shape, a.dtype) for a in operands] + [dma((len(operands),))]
    scratch += [
        pltpu.VMEM((2, 2, rows + 2, total, cols), BF16),
        pltpu.VMEM((2, 3 * chan, 3 * total), BF16),
        pltpu.VMEM((2, 2, rows, chan, cols), F32),
        pltpu.VMEM((2, 2, rows + 2, chan, cols), BF16),
        pltpu.VMEM((3, n_sp, 8, cols), F32),
        pltpu.VMEM((2, n_t, rows, 8, cols), F32),
        pltpu.VMEM((rows + 2, 8, cols), F32),
        pltpu.VMEM((2, n_sp, 8, cols), F32),
        pltpu.VMEM((3 * chan, latents * rows * cols), BF16),
        pltpu.VMEM((parts, deep, 3 * chan), BF16),
        pltpu.VMEM((n_dp, n_sp, deep, 3 * chan), BF16),
        pltpu.VMEM((n_dp, deep, 3 * chan), BF16),
        pltpu.VMEM((n_dp, deep, 3 * chan), BF16),
        pltpu.VMEM((n_sp, 40, chan), F32),
        pltpu.VMEM((n_dp, 40, chan), F32),
    ]
    for shape in (
        (2, 2, far), (2, 2, n_t), (3, near), (2, 2), (2, far), (2,), (2, near),
        (n_dp, near), (max(n_dp - 1, 1),), (near,), (max(n_dp - 1, 1),),
    ):
        scratch += [dma(shape), dma(shape)]
    dims = (n_dp, n_sp, n_t, rows, cols, chan, out_ch)
    logit, gw1, gw2 = pl.pallas_call(
        functools.partial(kernel, dims),
        out_shape=[
            jax.ShapeDtypeStruct((1, cols), F32),
            jax.ShapeDtypeStruct((9, piece, chan), F32),
            jax.ShapeDtypeStruct((9, out_ch, chan), F32),
        ],
        in_specs=[pl.BlockSpec(memory_space=pltpu.HBM)] * 14 + [SM] * 2,
        out_specs=[VM] * 3,
        scratch_shapes=scratch,
        compiler_params=pltpu.CompilerParams(
            collective_id=0, has_side_effects=True, vmem_limit_bytes=60 * 1024 * 1024
        ),
        name="dpo",
    )(*operands, timestep, winner)
    return logit[0, :1], gw1.transpose(0, 2, 1), gw2


def solution(mesh):
    in_specs = (
        P("dp", None, "tensor", "space", None),
        P("dp", None, "tensor", "space", None),
        P("dp", None, None, "space", None),
        P(None, "tensor", None),
        P(None, "tensor", None),
        P("tensor"),
        P("tensor"),
        P("tensor"),
        P("tensor"),
        P("tensor"),
        P("tensor"),
        P(None, None, "tensor"),
        P(None, None, "tensor"),
        P(None, "tensor"),
        P("dp"),
        P("dp"),
    )
    out_specs = (P("dp"), P(None, "tensor", ("dp", "space")), P(None, None, "tensor"))
    return jax.shard_map(body, mesh=mesh, in_specs=in_specs, out_specs=out_specs, check_vma=False)
```

```python
import functools

import jax
import jax.numpy as jnp
from jax import lax
from jax.experimental import pallas as pl
from jax.experimental.pallas import tpu as pltpu
from jax.sharding import PartitionSpec as P

GROUPS = 32
BETA = 500.0
EPS = 1e-05
F32 = jnp.float32
BF16 = jnp.bfloat16
VM = pl.BlockSpec(memory_space=pltpu.VMEM)
SM = pl.BlockSpec(memory_space=pltpu.SMEM)


def flip_bit(index, bit):
    return index + bit - 2 * bit * ((index // bit) % 2)


def dot_nt(a, b):
    return lax.dot_general(a, b, (((1,), (1,)), ((), ())), preferred_element_type=F32)


def shift_right(v, lane):
    return jnp.where(lane == 0, 0.0, pltpu.roll(v, 1, 1))


def shift_left(v, lane):
    cols = v.shape[1]
    return jnp.where(lane == cols - 1, 0.0, pltpu.roll(v, cols - 1, 1))


def kernel(
    dims,
    *refs,
):
    far_in, (timestep, winner, logit_out, gw1_out, gw2_out) = refs[:14], refs[14:19]
    near_in, load_sem = refs[19:33], refs[33]
    (
        x_buf, w1_all, pre, back, hid, stat, pred, edges, nz, res, err, d3, gsend, grecv, zsend, zrecv, w2x, w2z,
        fs, fr, hs, hr, ss, sr, es, er, ps, pr, rs, rr, qs, qr, gs, gr, zs, zr, ws, wr, vs, vr, ns, nr,
    ) = refs[34:]
    (
        feat_p, feat_r, noise, w1_p, w1_r, b1_p, b1_r, gain_p, bias_p, gain_r, bias_r,
        w2_p, w2_r, table,
    ) = near_in
    loads = [
        pltpu.make_async_copy(a, b, load_sem.at[k])
        for k, (a, b) in enumerate(zip(far_in, near_in))
    ]
    for c in loads:
        c.start()
    n_dp, n_sp, n_t, rows, cols, chan, out_ch = dims
    total = chan * n_t
    parts = n_dp * n_sp
    piece = total // parts
    group = total // GROUPS
    half = rows * cols
    d = lax.axis_index("dp")
    s = lax.axis_index("space")
    t = lax.axis_index("tensor")
    me = d * n_sp + s
    own = pl.ds(pl.multiple_of(t * chan, 16), chan)

    def at(dd=0, ds=0, dt=0):
        return {
            "dp": lax.rem(d + dd, n_dp),
            "space": lax.rem(s + ds + n_sp, n_sp),
            "tensor": lax.rem(t + dt, n_t),
        }

    def remote(src, dst, send, recv, device):
        return pltpu.make_async_remote_copy(
            src_ref=src, dst_ref=dst, send_sem=send, recv_sem=recv,
            device_id=device, device_id_type=pl.DeviceIdType.MESH,
        )

    partners = [(0, ds, dt) for ds in range(n_sp) for dt in range(n_t) if (ds, dt) != (0, 0)]
    partners += [(dd, 0, 0) for dd in range(1, n_dp)]
    barrier = pltpu.get_barrier_semaphore()
    for off in partners:
        pl.semaphore_signal(barrier, inc=1, device_id=at(*off), device_id_type=pl.DeviceIdType.MESH)

    ch_i = lax.broadcasted_iota(jnp.int32, (chan, chan * rows), 0)
    ch_j = lax.broadcasted_iota(jnp.int32, (chan, chan * rows), 1)
    order = jnp.concatenate(
        [jnp.where(ch_j == rows * ch_i + y, 1.0, 0.0) for y in range(rows)], axis=0
    ).astype(BF16)
    for m, feat in enumerate((feat_p, feat_r)):
        loads[m].wait()
        for i in range(2):
            rowwise = jnp.dot(order, feat[i], preferred_element_type=F32).astype(BF16)
            for y in range(rows):
                x_buf[m, i, 1 + y, own, :] = rowwise[y * chan : (y + 1) * chan]

    @pl.when(s == 0)
    def _():
        x_buf[:, :, 0] = jnp.zeros((2, 2, total, cols), BF16)
        hid[:, :, 0] = jnp.zeros((2, 2, chan, cols), BF16)
        res[0] = jnp.zeros((8, cols), F32)

    @pl.when(s == n_sp - 1)
    def _():
        x_buf[:, :, rows + 1] = jnp.zeros((2, 2, total, cols), BF16)
        hid[:, :, rows + 1] = jnp.zeros((2, 2, chan, cols), BF16)
        res[rows + 1] = jnp.zeros((8, cols), F32)

    stat[...] = jnp.zeros(stat.shape, F32)
    pl.semaphore_wait(barrier, len(partners))

    def halo(down, up):
        def start():
            @pl.when(s < n_sp - 1)
            def _():
                for c in down:
                    c.start()

            @pl.when(s > 0)
            def _():
                for c in up:
                    c.start()

        def arrive():
            @pl.when(s > 0)
            def _():
                for c in down:
                    c.wait_recv()

            @pl.when(s < n_sp - 1)
            def _():
                for c in up:
                    c.wait_recv()

        def finish():
            @pl.when(s < n_sp - 1)
            def _():
                for c in down:
                    c.wait_send()

            @pl.when(s > 0)
            def _():
                for c in up:
                    c.wait_send()

        return start, arrive, finish

    def feat_block(m, i, x):
        low = x & -x
        block = t
        bit = 1
        while bit < n_t:
            if (x ^ low) & bit:
                block = flip_bit(block, bit)
            bit *= 2
        spot = x_buf.at[m, i, pl.ds(1, rows), pl.ds(pl.multiple_of(block * chan, 16), chan), :]
        target = {"dp": d, "space": s, "tensor": flip_bit(t, low)}
        return remote(spot, spot, fs.at[m, i, x - 1], fr.at[m, i, x - 1], target)

    steps = sorted(range(1, n_t), key=lambda x: (bin(x).count("1"), -x))
    blocks = {(m, i, x): feat_block(m, i, x) for m in range(2) for i in range(2) for x in steps}
    feat_halo = []
    for m in range(2):
        down, up = [], []
        for dt in range(n_t):
            for go, ds, a, b, k in ((down, 1, rows, 0, 0), (up, -1, 1, rows + 1, 1)):
                go.append(remote(
                    x_buf.at[m, :, a, own, :], x_buf.at[m, :, b, own, :],
                    hs.at[m, k, dt], hr.at[m, k, dt], at(0, ds, dt),
                ))
        feat_halo.append(halo(down, up))

    def send_features(m):
        for i in range(2):
            for x in steps:
                if x & (x - 1) == 0:
                    blocks[m, i, x].start()
        feat_halo[m][0]()

    send_features(0)

    def forward(m):
        seen = set()
        for x in steps:
            if x & (x - 1):
                prior = x & (x - 1)
                for i in range(2):
                    if (i, prior) not in seen:
                        blocks[m, i, prior].wait_recv()
                        seen.add((i, prior))
                    blocks[m, i, x].start()
        return seen

    def gathered(m, i, seen):
        for x in steps:
            if (i, x) not in seen:
                blocks[m, i, x].wait_recv()
        if i == 0:
            feat_halo[m][1]()

    for c in loads[2:]:
        c.wait()
    for m, w1 in enumerate((w1_p, w1_r)):
        w1_all[m] = jnp.concatenate(
            [w1[3 * ky : 3 * ky + 3].reshape(3 * chan, total) for ky in range(3)], axis=1
        )

    ii = lax.broadcasted_iota(jnp.int32, (chan, chan), 0)
    jj = lax.broadcasted_iota(jnp.int32, (chan, chan), 1)
    eye = ii == jj
    same = jnp.zeros((chan, chan), F32)
    for g in range(chan // group):
        lo, hi = g * group, (g + 1) * group
        same += jnp.where((ii >= lo) & (ii < hi) & (jj >= lo) & (jj < hi), 1.0, 0.0)
    lane = lax.broadcasted_iota(jnp.int32, (chan, cols), 1)
    lane8 = lax.broadcasted_iota(jnp.int32, (8, cols), 1)
    lane24 = lax.broadcasted_iota(jnp.int32, (8, cols), 0)

    def column(row):
        return jnp.sum(jnp.where(eye, row, 0.0), axis=1, keepdims=True)

    def group_row(col):
        return jnp.sum(same * col, axis=0, keepdims=True)

    step_i = lax.broadcasted_iota(jnp.int32, table.shape, 1)
    shift = jnp.sum(jnp.where(step_i == timestep[0], table[...], 0.0), axis=1, keepdims=True)
    add = [column(b[...]) + shift for b in (b1_p, b1_r)]
    gain = [column(v[...]) for v in (gain_p, gain_r)]
    bias = [column(v[...]) for v in (bias_p, bias_r)]
    count = float(group * rows * n_sp * cols)

    def spread(k):
        copies = [
            remote(stat.at[k, s], stat.at[k, s], ss.at[k, o - 1], sr.at[k, o - 1], at(0, o))
            for o in range(1, n_sp)
        ]
        for c in copies:
            c.start()
        return copies

    def tally(k, lists):
        for i in range(2):
            for j in range(2):
                stat[k, s, 2 * i + j : 2 * i + j + 1, 0:chan] = group_row(lists[i][j])
        return spread(k)

    def collect(k, copies):
        for c in copies:
            c.wait_recv()
        sums = stat[k, 0]
        for o in range(1, n_sp):
            sums = sums + stat[k, o]
        sums = sums * (1.0 / count)
        return [[column(sums[2 * i + j : 2 * i + j + 1, 0:chan]) for j in range(2)] for i in range(2)]

    def window(m, i, which=slice(None)):
        return jnp.concatenate(
            [
                jnp.concatenate([x_buf[m, i, ky + y, which] for y in range(rows)], axis=1)
                for ky in range(3)
            ],
            axis=0,
        )

    def first_conv(m, seen):
        lists = []
        for i in range(2):
            gathered(m, i, seen)
            acc = jnp.dot(w1_all[m], window(m, i), preferred_element_type=F32)
            sums = jnp.zeros((chan, cols), F32)
            squares = jnp.zeros((chan, cols), F32)
            for y in range(rows):
                cut = slice(y * cols, (y + 1) * cols)
                v = acc[chan : 2 * chan, cut] + add[m]
                v = v + shift_right(acc[0:chan, cut], lane)
                v = v + shift_left(acc[2 * chan :, cut], lane)
                pre[m, i, 1 + y] = v
                sums = sums + v
                squares = squares + v * v
            lists.append([
                jnp.sum(sums, axis=1, keepdims=True), jnp.sum(squares, axis=1, keepdims=True)
            ])
        copies = tally(m, lists)
        sides = edge(lambda r: pre.at[m, :, r], es.at[m], er.at[m])
        sides[0]()
        return copies, sides

    def edge(buf, send, recv):
        down = [remote(buf(rows), buf(0), send.at[0], recv.at[0], at(0, 1))]
        up = [remote(buf(1), buf(rows + 1), send.at[1], recv.at[1], at(0, -1))]
        return halo(down, up)

    moments = [None, None]

    def activate(m, waits):
        copies, sides = waits
        sums = collect(m, copies)
        moments[m] = []
        for i in range(2):
            mean, square = sums[i]
            moments[m].append((mean, lax.rsqrt(square - mean * mean + EPS)))

        def rows_of(first, last):
            for i in range(2):
                mean, inv = moments[m][i]
                for r in range(first, last):
                    normed = (pre[m, i, r] - mean) * inv * gain[m] + bias[m]
                    hid[m, i, r] = (normed * jax.nn.sigmoid(normed)).astype(BF16)

        rows_of(1, rows + 1)
        sides[1]()

        @pl.when(s > 0)
        def _():
            rows_of(0, 1)

        @pl.when(s < n_sp - 1)
        def _():
            rows_of(rows + 1, rows + 2)

    zero4 = jnp.zeros((8 - out_ch, chan), F32)

    def taps_of(w2):
        first, second = [], []
        for k in range(9):
            w = w2[k].astype(F32)
            first += [w, zero4]
            second += [zero4, w]
        return jnp.concatenate(first, axis=0), jnp.concatenate(second, axis=0)

    taps2 = [taps_of(w2_p), taps_of(w2_r)]

    def second_conv(m):
        acc = None
        for i in range(2):
            cells = jnp.concatenate([hid[m, i, r] for r in range(rows + 2)], axis=1)
            term = jnp.dot(taps2[m][i].astype(BF16), cells, preferred_element_type=F32)
            acc = term if acc is None else acc + term
        for y in range(rows):
            by_kx = []
            for kx in range(3):
                v = None
                for ky in range(3):
                    k = 3 * ky + kx
                    term = acc[8 * k : 8 * k + 8, (y + ky) * cols : (y + ky + 1) * cols]
                    v = term if v is None else v + term
                by_kx.append(v)
            pred[m, t, y] = by_kx[1] + shift_right(by_kx[0], lane8) + shift_left(by_kx[2], lane8)
        copies = [
            remote(pred.at[m, t], pred.at[m, t], ps.at[m, o - 1], pr.at[m, o - 1], at(0, 0, o))
            for o in range(1, n_t)
        ]
        if m == 0:
            pred_edge[0]()
        for c in copies:
            c.start()
        return copies

    def residual(m, copies):
        for c in copies:
            c.wait_recv()
        squares = jnp.zeros((8, cols), F32)
        for y in range(rows):
            v = pred[m, 0, y]
            for o in range(1, n_t):
                v = v + pred[m, o, y]
            v = v - nz[1 + y]
            squares = squares + v * v
            if m == 0:
                res[1 + y] = v
        err[m, s] = jnp.broadcast_to(jnp.sum(squares, axis=1, keepdims=True), (8, cols))
        sends = [
            remote(err.at[m, s], err.at[m, s], qs.at[m, o - 1], qr.at[m, o - 1], at(0, o))
            for o in range(1, n_sp)
        ]
        for c in sends:
            c.start()
        return sends

    down, up = [], []
    for dt in range(n_t):
        for go, ds, a, k in ((down, 1, rows - 1, 0), (up, -1, 0, 1)):
            go.append(remote(
                pred.at[0, t, a], edges.at[k, t], rs.at[k, dt], rr.at[k, dt], at(0, ds, dt)
            ))
    pred_edge = halo(down, up)

    def edge_residual(k, r):
        v = edges[k, 0]
        for o in range(1, n_t):
            v = v + edges[k, o]
        res[r] = v - nz[r]

    pending = []
    for y in range(rows):
        nz[1 + y] = noise[:, y, :]
    noise_edge = edge(lambda r: nz.at[r], ns, nr)
    noise_edge[0]()

    seen = forward(0)
    send_features(1)
    stat_p = first_conv(0, seen)
    activate(0, stat_p)
    pred_p = second_conv(0)
    seen = forward(1)
    stat_r = first_conv(1, seen)
    err_p = residual(0, pred_p)
    noise_edge[1]()
    pred_edge[1]()

    @pl.when(s > 0)
    def _():
        edge_residual(0, 0)

    @pl.when(s < n_sp - 1)
    def _():
        edge_residual(1, rows + 1)

    sign = jnp.where(lane24 < 4, 1.0, -1.0)
    rows3 = []
    for r in range(rows + 2):
        v = res[r] * sign
        v = v.astype(BF16).astype(F32)
        rows3.append(jnp.concatenate([shift_left(v, lane8), v, shift_right(v, lane8)], axis=0))
    spread9 = jnp.concatenate(
        [jnp.concatenate([rows3[y + 2 - ky] for y in range(rows)], axis=1) for ky in range(3)], axis=0
    ).astype(BF16)
    lists = []
    for i in range(2):
        mean, inv = moments[0][i]
        flipped = jnp.transpose(taps2[0][i]).astype(BF16)
        dh = jnp.dot(flipped, spread9, preferred_element_type=F32)
        first = jnp.zeros((chan, cols), F32)
        second = jnp.zeros((chan, cols), F32)
        for y in range(rows):
            xhat = (pre[0, i, 1 + y] - mean) * inv
            normed = xhat * gain[0] + bias[0]
            gate = jax.nn.sigmoid(normed)
            g = dh[:, y * cols : (y + 1) * cols] * gate * (1.0 + normed * (1.0 - gate)) * gain[0]
            first = first + g
            second = second + g * xhat
            back[0, i, y] = xhat
            back[1, i, y] = g
        lists.append([jnp.sum(first, axis=1, keepdims=True), jnp.sum(second, axis=1, keepdims=True)])
    stat_b = tally(2, lists)
    activate(1, stat_r)
    pred_r = second_conv(1)

    center = jnp.concatenate(rows3[1 : rows + 1], axis=1)
    half_row = lax.broadcasted_iota(jnp.int32, center.shape, 0)
    in_first = (half_row % 8) < 4
    w2_sum = [None] * 3
    for i in range(2):
        mine = jnp.where(in_first if i == 0 else jnp.logical_not(in_first), center, 0.0).astype(BF16)
        for ky in range(3):
            cells = jnp.concatenate([hid[0, i, ky + y] for y in range(rows)], axis=1)
            term = dot_nt(mine, cells)
            w2_sum[ky] = term if w2_sum[ky] is None else w2_sum[ky] + term

    taps = [w2_sum[k // 3][8 * (k % 3) : 8 * (k % 3) + 8] for k in range(9)]
    taps = [v + pltpu.roll(v, 4, 0) for v in taps] + [jnp.zeros((8, chan), F32)]
    upper = lax.broadcasted_iota(jnp.int32, (8, chan), 0) < 4
    for j in range(5):
        w2x[s, 8 * j : 8 * j + 8] = jnp.where(upper, taps[2 * j], taps[2 * j + 1])
    w2_near = [
        remote(w2x.at[s], w2x.at[s], ws.at[o - 1], wr.at[o - 1], at(0, o)) for o in range(1, n_sp)
    ]
    for c in w2_near:
        c.start()

    sums = collect(2, stat_b)
    for i in range(2):
        a, b = sums[i]
        inv = moments[0][i][1]
        for y in range(rows):
            v = inv * (back[1, i, y] - a - back[0, i, y] * b)
            cut = slice((i * rows + y) * cols, (i * rows + y + 1) * cols)
            d3[0:chan, cut] = shift_left(v, lane).astype(BF16)
            d3[chan : 2 * chan, cut] = v.astype(BF16)
            d3[2 * chan : 3 * chan, cut] = shift_right(v, lane).astype(BF16)

    unit = piece * n_sp
    spare = gsend.shape[1] - 3 * piece

    def gradient(which, width, first):
        cells = jnp.concatenate([window(0, i, which) for i in range(2)], axis=1)
        grads = dot_nt(cells, d3[...])
        for p in range(width // piece):
            block = [grads[ky * width + p * piece : ky * width + (p + 1) * piece] for ky in range(3)]
            if spare:
                block.append(jnp.zeros((spare, 3 * chan), F32))
            gsend[first + p] = jnp.concatenate(block, axis=0).astype(BF16)

    if unit % 16:
        gradient(slice(None), total, 0)
    order_dp = sorted(range(1, n_dp), key=lambda o: -min(o, n_dp - o)) + [0]
    g_near = {}
    for dd in order_dp:
        there = lax.rem(d + dd, n_dp)
        if unit % 16 == 0:
            gradient(pl.ds(pl.multiple_of(there * unit, 16), unit), unit, there * n_sp)
        for o in range(1, n_sp):
            target = there * n_sp + lax.rem(s + o, n_sp)
            c = remote(
                gsend.at[target], grecv.at[there, s], gs.at[dd, o - 1], gr.at[dd, o - 1], at(0, o)
            )
            c.start()
            g_near[dd, o] = c

    err_r = residual(1, pred_r)
    for c in err_p + err_r:
        c.wait_recv()
    gaps = []
    for m in range(2):
        v = err[m, 0]
        for o in range(1, n_sp):
            v = v + err[m, o]
        v = v * (1.0 / (out_ch * half * n_sp))
        gaps.append(jnp.sum(v * sign, axis=0, keepdims=True))
    pair_sign = 1.0 - 2.0 * winner[0].astype(F32)
    logit = (-0.5 * BETA) * pair_sign * (gaps[0] - gaps[1])
    logit_out[...] = logit
    factor = (BETA / (out_ch * half * n_sp)) * pair_sign * jax.nn.sigmoid(-logit)[:, 0:1]

    for c in w2_near:
        c.wait_recv()
    v = w2x[0]
    for o in range(1, n_sp):
        v = v + w2x[o]
    w2z[d] = v * factor
    w2_far = [
        remote(w2z.at[d], w2z.at[d], vs.at[dd - 1], vr.at[dd - 1], at(dd)) for dd in range(1, n_dp)
    ]
    for c in w2_far:
        c.start()

    g_far = []
    mine = None
    for dd in order_dp:
        there = lax.rem(d + dd, n_dp)
        v = gsend[there * n_sp + s].astype(F32)
        for o in range(1, n_sp):
            g_near[dd, o].wait_recv()
            v = v + grecv[there, lax.rem(s + n_sp - o, n_sp)].astype(F32)
        v = v * factor
        if dd == 0:
            mine = v
        else:
            zsend[there] = v.astype(BF16)
            c = remote(zsend.at[there], zrecv.at[d], zs.at[dd - 1], zr.at[dd - 1], at(dd))
            c.start()
            g_far.append(c)

    for c in w2_far:
        c.wait_recv()
    v = w2z[0]
    for o in range(1, n_dp):
        v = v + w2z[o]
    for k in range(9):
        gw2_out[k] = v[4 * k : 4 * k + 4]

    for c in g_far:
        c.wait_recv()
    for dd in range(1, n_dp):
        mine = mine + zrecv[lax.rem(d + dd, n_dp)].astype(F32)
    for ky in range(3):
        for kx in range(3):
            gw1_out[3 * ky + kx] = mine[ky * piece : (ky + 1) * piece, kx * chan : (kx + 1) * chan]

    for c in blocks.values():
        c.wait_send()
    for sides in (feat_halo[0], feat_halo[1], stat_p[1], stat_r[1], noise_edge, pred_edge):
        sides[2]()
    for c in stat_p[0] + stat_r[0] + stat_b + pred_p + pred_r + err_p + err_r + w2_near + w2_far + g_far:
        c.wait_send()
    for c in g_near.values():
        c.wait_send()


def hand_over(first, second, first_out, second_out, sems):
    copies = [
        pltpu.make_async_copy(first, first_out, sems.at[0]),
        pltpu.make_async_copy(second, second_out, sems.at[1]),
    ]
    for c in copies:
        c.start()
    for c in copies:
        c.wait()


def body(
    feat_policy, feat_ref, noise, w1_policy, w1_ref, b1_policy, b1_ref,
    gn_gain_policy, gn_bias_policy, gn_gain_ref, gn_bias_ref,
    w2_policy, w2_ref, time_table, timestep, winner,
):
    _, latents, chan, rows, cols = feat_policy.shape
    out_ch = noise.shape[2]
    n_dp, n_sp, n_t = (lax.axis_size(a) for a in ("dp", "space", "tensor"))
    total, parts = chan * n_t, n_dp * n_sp
    piece = total // parts
    deep = -(-3 * piece // 16) * 16
    dma = pltpu.SemaphoreType.DMA
    near, far = max(n_sp - 1, 1), max(n_t - 1, 1)
    operands = [
        feat_policy.reshape(latents, chan * rows, cols),
        feat_ref.reshape(latents, chan * rows, cols),
        noise.reshape(latents * out_ch, rows, cols),
        w1_policy, w1_ref,
        b1_policy[None], b1_ref[None],
        gn_gain_policy[None], gn_bias_policy[None], gn_gain_ref[None], gn_bias_ref[None],
        w2_policy, w2_ref, time_table.T,
    ]
    scratch = [pltpu.VMEM(a.shape, a.dtype) for a in operands] + [dma((len(operands),))]
    scratch += [
        pltpu.VMEM((2, 2, rows + 2, total, cols), BF16),
        pltpu.VMEM((2, 3 * chan, 3 * total), BF16),
        pltpu.VMEM((2, 2, rows + 2, chan, cols), F32),
        pltpu.VMEM((2, 2, rows, chan, cols), F32),
        pltpu.VMEM((2, 2, rows + 2, chan, cols), BF16),
        pltpu.VMEM((3, n_sp, 8, cols), F32),
        pltpu.VMEM((2, n_t, rows, 8, cols), F32),
        pltpu.VMEM((2, n_t, 8, cols), F32),
        pltpu.VMEM((rows + 2, 8, cols), F32),
        pltpu.VMEM((rows + 2, 8, cols), F32),
        pltpu.VMEM((2, n_sp, 8, cols), F32),
        pltpu.VMEM((3 * chan, latents * rows * cols), BF16),
        pltpu.VMEM((parts, deep, 3 * chan), BF16),
        pltpu.VMEM((n_dp, n_sp, deep, 3 * chan), BF16),
        pltpu.VMEM((n_dp, deep, 3 * chan), BF16),
        pltpu.VMEM((n_dp, deep, 3 * chan), BF16),
        pltpu.VMEM((n_sp, 40, chan), F32),
        pltpu.VMEM((n_dp, 40, chan), F32),
    ]
    for shape in (
        (2, 2, far), (2, 2, n_t), (3, near), (2, 2), (2, far), (2, n_t), (2, near),
        (n_dp, near), (max(n_dp - 1, 1),), (near,), (max(n_dp - 1, 1),), (2,),
    ):
        scratch += [dma(shape), dma(shape)]
    dims = (n_dp, n_sp, n_t, rows, cols, chan, out_ch)
    logit, gw1, gw2 = pl.pallas_call(
        functools.partial(kernel, dims),
        out_shape=[
            jax.ShapeDtypeStruct((1, cols), F32),
            jax.ShapeDtypeStruct((9, piece, chan), F32),
            jax.ShapeDtypeStruct((9, out_ch, chan), F32),
        ],
        in_specs=[pl.BlockSpec(memory_space=pltpu.HBM)] * 14 + [SM] * 2,
        out_specs=[VM] * 3,
        scratch_shapes=scratch,
        compiler_params=pltpu.CompilerParams(
            collective_id=0, has_side_effects=True, vmem_limit_bytes=60 * 1024 * 1024
        ),
        name="dpo",
    )(*operands, timestep, winner)
    gw1, gw2 = pl.pallas_call(
        hand_over,
        out_shape=[jax.ShapeDtypeStruct(a.shape, a.dtype) for a in (gw1, gw2)],
        in_specs=[pl.BlockSpec(memory_space=pl.ANY)] * 2,
        out_specs=[pl.BlockSpec(memory_space=pl.ANY)] * 2,
        scratch_shapes=[dma((2,))],
        compiler_params=pltpu.CompilerParams(vmem_limit_bytes=60 * 1024 * 1024),
        name="hand_over",
    )(gw1, gw2)
    return logit[0, :1], gw1.transpose(0, 2, 1), gw2


def solution(mesh):
    in_specs = (
        P("dp", None, "tensor", "space", None),
        P("dp", None, "tensor", "space", None),
        P("dp", None, None, "space", None),
        P(None, "tensor", None),
        P(None, "tensor", None),
        P("tensor"),
        P("tensor"),
        P("tensor"),
        P("tensor"),
        P("tensor"),
        P("tensor"),
        P(None, None, "tensor"),
        P(None, None, "tensor"),
        P(None, "tensor"),
        P("dp"),
        P("dp"),
    )
    out_specs = (P("dp"), P(None, "tensor", ("dp", "space")), P(None, None, "tensor"))
    return jax.shard_map(body, mesh=mesh, in_specs=in_specs, out_specs=out_specs, check_vma=False)
```

```python
import functools

import jax
import jax.numpy as jnp
from jax import lax
from jax.experimental import pallas as pl
from jax.experimental.pallas import tpu as pltpu
from jax.sharding import PartitionSpec as P

GROUPS = 32
BETA = 500.0
EPS = 1e-05
F32 = jnp.float32
BF16 = jnp.bfloat16
VM = pl.BlockSpec(memory_space=pltpu.VMEM)
SM = pl.BlockSpec(memory_space=pltpu.SMEM)


def flip_bit(index, bit):
    return index + bit - 2 * bit * ((index // bit) % 2)


def dot_nt(a, b):
    return lax.dot_general(a, b, (((1,), (1,)), ((), ())), preferred_element_type=F32)


def shift_right(v, lane):
    return jnp.where(lane == 0, 0.0, pltpu.roll(v, 1, 1))


def shift_left(v, lane):
    cols = v.shape[1]
    return jnp.where(lane == cols - 1, 0.0, pltpu.roll(v, cols - 1, 1))


def kernel(
    dims,
    *refs,
):
    far_in, (timestep, winner, logit_out, gw1_out, gw2_out) = refs[:14], refs[14:19]
    near_in, load_sem = refs[19:33], refs[33]
    (
        x_buf, w1_all, pre, back, hid, stat, pred, edges, nz, res, err, d3, gsend, grecv, zsend, zrecv, w2x, w2z,
        fs, fr, hs, hr, ss, sr, es, er, ps, pr, rs, rr, qs, qr, gs, gr, zs, zr, ws, wr, vs, vr, ns, nr,
    ) = refs[34:]
    (
        feat_p, feat_r, noise, w1_p, w1_r, b1_p, b1_r, gain_p, bias_p, gain_r, bias_r,
        w2_p, w2_r, table,
    ) = near_in
    loads = [
        pltpu.make_async_copy(a, b, load_sem.at[k])
        for k, (a, b) in enumerate(zip(far_in, near_in))
    ]
    for c in loads:
        c.start()
    n_dp, n_sp, n_t, rows, cols, chan, out_ch = dims
    total = chan * n_t
    parts = n_dp * n_sp
    piece = total // parts
    group = total // GROUPS
    half = rows * cols
    d = lax.axis_index("dp")
    s = lax.axis_index("space")
    t = lax.axis_index("tensor")
    me = d * n_sp + s
    own = pl.ds(pl.multiple_of(t * chan, 16), chan)

    def at(dd=0, ds=0, dt=0):
        return {
            "dp": lax.rem(d + dd, n_dp),
            "space": lax.rem(s + ds + n_sp, n_sp),
            "tensor": lax.rem(t + dt, n_t),
        }

    def remote(src, dst, send, recv, device):
        return pltpu.make_async_remote_copy(
            src_ref=src, dst_ref=dst, send_sem=send, recv_sem=recv,
            device_id=device, device_id_type=pl.DeviceIdType.MESH,
        )

    partners = [(0, ds, dt) for ds in range(n_sp) for dt in range(n_t) if (ds, dt) != (0, 0)]
    partners += [(dd, 0, 0) for dd in range(1, n_dp)]
    barrier = pltpu.get_barrier_semaphore()
    for off in partners:
        pl.semaphore_signal(barrier, inc=1, device_id=at(*off), device_id_type=pl.DeviceIdType.MESH)

    ch_i = lax.broadcasted_iota(jnp.int32, (chan, chan * rows), 0)
    ch_j = lax.broadcasted_iota(jnp.int32, (chan, chan * rows), 1)
    order = jnp.concatenate(
        [jnp.where(ch_j == rows * ch_i + y, 1.0, 0.0) for y in range(rows)], axis=0
    ).astype(BF16)
    for m, feat in enumerate((feat_p, feat_r)):
        loads[m].wait()
        for i in range(2):
            rowwise = jnp.dot(order, feat[i], preferred_element_type=F32).astype(BF16)
            for y in range(rows):
                x_buf[m, i, 1 + y, own, :] = rowwise[y * chan : (y + 1) * chan]

    @pl.when(s == 0)
    def _():
        x_buf[:, :, 0] = jnp.zeros((2, 2, total, cols), BF16)
        hid[:, :, 0] = jnp.zeros((2, 2, chan, cols), BF16)
        res[0] = jnp.zeros((8, cols), F32)

    @pl.when(s == n_sp - 1)
    def _():
        x_buf[:, :, rows + 1] = jnp.zeros((2, 2, total, cols), BF16)
        hid[:, :, rows + 1] = jnp.zeros((2, 2, chan, cols), BF16)
        res[rows + 1] = jnp.zeros((8, cols), F32)

    stat[...] = jnp.zeros(stat.shape, F32)
    pl.semaphore_wait(barrier, len(partners))

    def halo(down, up):
        def start():
            @pl.when(s < n_sp - 1)
            def _():
                for c in down:
                    c.start()

            @pl.when(s > 0)
            def _():
                for c in up:
                    c.start()

        def arrive():
            @pl.when(s > 0)
            def _():
                for c in down:
                    c.wait_recv()

            @pl.when(s < n_sp - 1)
            def _():
                for c in up:
                    c.wait_recv()

        def finish():
            @pl.when(s < n_sp - 1)
            def _():
                for c in down:
                    c.wait_send()

            @pl.when(s > 0)
            def _():
                for c in up:
                    c.wait_send()

        return start, arrive, finish

    def feat_block(m, i, x):
        low = x & -x
        block = t
        bit = 1
        while bit < n_t:
            if (x ^ low) & bit:
                block = flip_bit(block, bit)
            bit *= 2
        spot = x_buf.at[m, i, pl.ds(1, rows), pl.ds(pl.multiple_of(block * chan, 16), chan), :]
        target = {"dp": d, "space": s, "tensor": flip_bit(t, low)}
        return remote(spot, spot, fs.at[m, i, x - 1], fr.at[m, i, x - 1], target)

    steps = sorted(range(1, n_t), key=lambda x: (bin(x).count("1"), -x))
    blocks = {(m, i, x): feat_block(m, i, x) for m in range(2) for i in range(2) for x in steps}
    feat_halo = []
    for m in range(2):
        down, up = [], []
        for dt in range(n_t):
            for go, ds, a, b, k in ((down, 1, rows, 0, 0), (up, -1, 1, rows + 1, 1)):
                go.append(remote(
                    x_buf.at[m, :, a, own, :], x_buf.at[m, :, b, own, :],
                    hs.at[m, k, dt], hr.at[m, k, dt], at(0, ds, dt),
                ))
        feat_halo.append(halo(down, up))

    def send_features(m):
        for i in range(2):
            for x in steps:
                if x & (x - 1) == 0:
                    blocks[m, i, x].start()
        feat_halo[m][0]()

    send_features(0)

    def forward(m):
        seen = set()
        for x in steps:
            if x & (x - 1):
                prior = x & (x - 1)
                for i in range(2):
                    if (i, prior) not in seen:
                        blocks[m, i, prior].wait_recv()
                        seen.add((i, prior))
                    blocks[m, i, x].start()
        return seen

    def gathered(m, i, seen):
        for x in steps:
            if (i, x) not in seen:
                blocks[m, i, x].wait_recv()
        if i == 0:
            feat_halo[m][1]()

    for c in loads[2:]:
        c.wait()
    for m, w1 in enumerate((w1_p, w1_r)):
        w1_all[m] = jnp.concatenate(
            [w1[3 * ky : 3 * ky + 3].reshape(3 * chan, total) for ky in range(3)], axis=1
        )

    ii = lax.broadcasted_iota(jnp.int32, (chan, chan), 0)
    jj = lax.broadcasted_iota(jnp.int32, (chan, chan), 1)
    eye = ii == jj
    same = jnp.zeros((chan, chan), F32)
    for g in range(chan // group):
        lo, hi = g * group, (g + 1) * group
        same += jnp.where((ii >= lo) & (ii < hi) & (jj >= lo) & (jj < hi), 1.0, 0.0)
    lane = lax.broadcasted_iota(jnp.int32, (chan, cols), 1)
    lane8 = lax.broadcasted_iota(jnp.int32, (8, cols), 1)
    lane24 = lax.broadcasted_iota(jnp.int32, (8, cols), 0)

    def column(row):
        return jnp.sum(jnp.where(eye, row, 0.0), axis=1, keepdims=True)

    def group_row(col):
        return jnp.sum(same * col, axis=0, keepdims=True)

    step_i = lax.broadcasted_iota(jnp.int32, table.shape, 1)
    shift = jnp.sum(jnp.where(step_i == timestep[0], table[...], 0.0), axis=1, keepdims=True)
    add = [column(b[...]) + shift for b in (b1_p, b1_r)]
    gain = [column(v[...]) for v in (gain_p, gain_r)]
    bias = [column(v[...]) for v in (bias_p, bias_r)]
    count = float(group * rows * n_sp * cols)

    def spread(k):
        copies = [
            remote(stat.at[k, s], stat.at[k, s], ss.at[k, o - 1], sr.at[k, o - 1], at(0, o))
            for o in range(1, n_sp)
        ]
        for c in copies:
            c.start()
        return copies

    def tally(k, lists):
        for i in range(2):
            for j in range(2):
                stat[k, s, 2 * i + j : 2 * i + j + 1, 0:chan] = group_row(lists[i][j])
        return spread(k)

    def collect(k, copies):
        for c in copies:
            c.wait_recv()
        sums = stat[k, 0]
        for o in range(1, n_sp):
            sums = sums + stat[k, o]
        sums = sums * (1.0 / count)
        return [[column(sums[2 * i + j : 2 * i + j + 1, 0:chan]) for j in range(2)] for i in range(2)]

    def window(m, i, which=slice(None)):
        return jnp.concatenate(
            [
                jnp.concatenate([x_buf[m, i, ky + y, which] for y in range(rows)], axis=1)
                for ky in range(3)
            ],
            axis=0,
        )

    def first_conv(m, seen):
        lists = []
        for i in range(2):
            gathered(m, i, seen)
            acc = jnp.dot(w1_all[m], window(m, i), preferred_element_type=F32)
            sums = jnp.zeros((chan, cols), F32)
            squares = jnp.zeros((chan, cols), F32)
            for y in range(rows):
                cut = slice(y * cols, (y + 1) * cols)
                v = acc[chan : 2 * chan, cut] + add[m]
                v = v + shift_right(acc[0:chan, cut], lane)
                v = v + shift_left(acc[2 * chan :, cut], lane)
                pre[m, i, 1 + y] = v
                sums = sums + v
                squares = squares + v * v
            lists.append([
                jnp.sum(sums, axis=1, keepdims=True), jnp.sum(squares, axis=1, keepdims=True)
            ])
        copies = tally(m, lists)
        sides = edge(lambda r: pre.at[m, :, r], es.at[m], er.at[m])
        sides[0]()
        return copies, sides

    def edge(buf, send, recv):
        down = [remote(buf(rows), buf(0), send.at[0], recv.at[0], at(0, 1))]
        up = [remote(buf(1), buf(rows + 1), send.at[1], recv.at[1], at(0, -1))]
        return halo(down, up)

    moments = [None, None]

    def activate(m, waits):
        copies, sides = waits
        sums = collect(m, copies)
        moments[m] = []
        for i in range(2):
            mean, square = sums[i]
            moments[m].append((mean, lax.rsqrt(square - mean * mean + EPS)))

        def rows_of(first, last):
            for i in range(2):
                mean, inv = moments[m][i]
                for r in range(first, last):
                    normed = (pre[m, i, r] - mean) * inv * gain[m] + bias[m]
                    hid[m, i, r] = (normed * jax.nn.sigmoid(normed)).astype(BF16)

        rows_of(1, rows + 1)
        sides[1]()

        @pl.when(s > 0)
        def _():
            rows_of(0, 1)

        @pl.when(s < n_sp - 1)
        def _():
            rows_of(rows + 1, rows + 2)

    zero4 = jnp.zeros((8 - out_ch, chan), F32)

    def taps_of(w2):
        first, second = [], []
        for k in range(9):
            w = w2[k].astype(F32)
            first += [w, zero4]
            second += [zero4, w]
        return jnp.concatenate(first, axis=0), jnp.concatenate(second, axis=0)

    taps2 = [taps_of(w2_p), taps_of(w2_r)]

    def second_conv(m):
        acc = None
        for i in range(2):
            cells = jnp.concatenate([hid[m, i, r] for r in range(rows + 2)], axis=1)
            term = jnp.dot(taps2[m][i].astype(BF16), cells, preferred_element_type=F32)
            acc = term if acc is None else acc + term
        for y in range(rows):
            by_kx = []
            for kx in range(3):
                v = None
                for ky in range(3):
                    k = 3 * ky + kx
                    term = acc[8 * k : 8 * k + 8, (y + ky) * cols : (y + ky + 1) * cols]
                    v = term if v is None else v + term
                by_kx.append(v)
            pred[m, t, y] = by_kx[1] + shift_right(by_kx[0], lane8) + shift_left(by_kx[2], lane8)
        copies = [
            remote(pred.at[m, t], pred.at[m, t], ps.at[m, o - 1], pr.at[m, o - 1], at(0, 0, o))
            for o in range(1, n_t)
        ]
        if m == 0:
            pred_edge[0]()
        for c in copies:
            c.start()
        return copies

    def residual(m, copies):
        for c in copies:
            c.wait_recv()
        squares = jnp.zeros((8, cols), F32)
        for y in range(rows):
            v = pred[m, 0, y]
            for o in range(1, n_t):
                v = v + pred[m, o, y]
            v = v - nz[1 + y]
            squares = squares + v * v
            if m == 0:
                res[1 + y] = v
        err[m, s] = jnp.broadcast_to(jnp.sum(squares, axis=1, keepdims=True), (8, cols))
        sends = [
            remote(err.at[m, s], err.at[m, s], qs.at[m, o - 1], qr.at[m, o - 1], at(0, o))
            for o in range(1, n_sp)
        ]
        for c in sends:
            c.start()
        return sends

    down, up = [], []
    for dt in range(n_t):
        for go, ds, a, k in ((down, 1, rows - 1, 0), (up, -1, 0, 1)):
            go.append(remote(
                pred.at[0, t, a], edges.at[k, t], rs.at[k, dt], rr.at[k, dt], at(0, ds, dt)
            ))
    pred_edge = halo(down, up)

    def edge_residual(k, r):
        v = edges[k, 0]
        for o in range(1, n_t):
            v = v + edges[k, o]
        res[r] = v - nz[r]

    pending = []
    for y in range(rows):
        nz[1 + y] = noise[:, y, :]
    noise_edge = edge(lambda r: nz.at[r], ns, nr)
    noise_edge[0]()

    seen = forward(0)
    send_features(1)
    stat_p = first_conv(0, seen)
    activate(0, stat_p)
    pred_p = second_conv(0)
    seen = forward(1)
    stat_r = first_conv(1, seen)
    err_p = residual(0, pred_p)
    noise_edge[1]()
    pred_edge[1]()

    @pl.when(s > 0)
    def _():
        edge_residual(0, 0)

    @pl.when(s < n_sp - 1)
    def _():
        edge_residual(1, rows + 1)

    sign = jnp.where(lane24 < 4, 1.0, -1.0)
    rows3 = []
    for r in range(rows + 2):
        v = res[r] * sign
        v = v.astype(BF16).astype(F32)
        rows3.append(jnp.concatenate([shift_left(v, lane8), v, shift_right(v, lane8)], axis=0))
    spread9 = jnp.concatenate(
        [jnp.concatenate([rows3[y + 2 - ky] for y in range(rows)], axis=1) for ky in range(3)], axis=0
    ).astype(BF16)
    lists = []
    for i in range(2):
        mean, inv = moments[0][i]
        flipped = jnp.transpose(taps2[0][i]).astype(BF16)
        dh = jnp.dot(flipped, spread9, preferred_element_type=F32)
        first = jnp.zeros((chan, cols), F32)
        second = jnp.zeros((chan, cols), F32)
        for y in range(rows):
            xhat = (pre[0, i, 1 + y] - mean) * inv
            normed = xhat * gain[0] + bias[0]
            gate = jax.nn.sigmoid(normed)
            g = dh[:, y * cols : (y + 1) * cols] * gate * (1.0 + normed * (1.0 - gate)) * gain[0]
            first = first + g
            second = second + g * xhat
            back[0, i, y] = xhat
            back[1, i, y] = g
        lists.append([jnp.sum(first, axis=1, keepdims=True), jnp.sum(second, axis=1, keepdims=True)])
    stat_b = tally(2, lists)
    activate(1, stat_r)
    pred_r = second_conv(1)

    center = jnp.concatenate(rows3[1 : rows + 1], axis=1)
    half_row = lax.broadcasted_iota(jnp.int32, center.shape, 0)
    in_first = (half_row % 8) < 4
    w2_sum = [None] * 3
    for i in range(2):
        mine = jnp.where(in_first if i == 0 else jnp.logical_not(in_first), center, 0.0).astype(BF16)
        for ky in range(3):
            cells = jnp.concatenate([hid[0, i, ky + y] for y in range(rows)], axis=1)
            term = dot_nt(mine, cells)
            w2_sum[ky] = term if w2_sum[ky] is None else w2_sum[ky] + term

    taps = [w2_sum[k // 3][8 * (k % 3) : 8 * (k % 3) + 8] for k in range(9)]
    taps = [v + pltpu.roll(v, 4, 0) for v in taps] + [jnp.zeros((8, chan), F32)]
    upper = lax.broadcasted_iota(jnp.int32, (8, chan), 0) < 4
    for j in range(5):
        w2x[s, 8 * j : 8 * j + 8] = jnp.where(upper, taps[2 * j], taps[2 * j + 1])
    w2_near = [
        remote(w2x.at[s], w2x.at[s], ws.at[o - 1], wr.at[o - 1], at(0, o)) for o in range(1, n_sp)
    ]
    for c in w2_near:
        c.start()

    err_r = residual(1, pred_r)
    sums = collect(2, stat_b)
    for i in range(2):
        a, b = sums[i]
        inv = moments[0][i][1]
        for y in range(rows):
            v = inv * (back[1, i, y] - a - back[0, i, y] * b)
            cut = slice((i * rows + y) * cols, (i * rows + y + 1) * cols)
            d3[0:chan, cut] = shift_left(v, lane).astype(BF16)
            d3[chan : 2 * chan, cut] = v.astype(BF16)
            d3[2 * chan : 3 * chan, cut] = shift_right(v, lane).astype(BF16)

    unit = piece * n_sp
    spare = gsend.shape[1] - 3 * piece

    def gradient(which, width, first):
        cells = jnp.concatenate([window(0, i, which) for i in range(2)], axis=1)
        grads = dot_nt(cells, d3[...])
        for p in range(width // piece):
            block = [grads[ky * width + p * piece : ky * width + (p + 1) * piece] for ky in range(3)]
            if spare:
                block.append(jnp.zeros((spare, 3 * chan), F32))
            gsend[first + p] = jnp.concatenate(block, axis=0).astype(BF16)

    if unit % 16:
        gradient(slice(None), total, 0)
    order_dp = sorted(range(1, n_dp), key=lambda o: -min(o, n_dp - o)) + [0]
    g_near = {}
    for dd in order_dp:
        there = lax.rem(d + dd, n_dp)
        if unit % 16 == 0:
            gradient(pl.ds(pl.multiple_of(there * unit, 16), unit), unit, there * n_sp)
        for o in range(1, n_sp):
            target = there * n_sp + lax.rem(s + o, n_sp)
            c = remote(
                gsend.at[target], grecv.at[there, s], gs.at[dd, o - 1], gr.at[dd, o - 1], at(0, o)
            )
            c.start()
            g_near[dd, o] = c

    for c in err_p + err_r:
        c.wait_recv()
    gaps = []
    for m in range(2):
        v = err[m, 0]
        for o in range(1, n_sp):
            v = v + err[m, o]
        v = v * (1.0 / (out_ch * half * n_sp))
        gaps.append(jnp.sum(v * sign, axis=0, keepdims=True))
    pair_sign = 1.0 - 2.0 * winner[0].astype(F32)
    logit = (-0.5 * BETA) * pair_sign * (gaps[0] - gaps[1])
    logit_out[...] = logit
    factor = (BETA / (out_ch * half * n_sp)) * pair_sign * jax.nn.sigmoid(-logit)[:, 0:1]

    for c in w2_near:
        c.wait_recv()
    v = w2x[0]
    for o in range(1, n_sp):
        v = v + w2x[o]
    w2z[d] = v * factor
    w2_far = [
        remote(w2z.at[d], w2z.at[d], vs.at[dd - 1], vr.at[dd - 1], at(dd)) for dd in range(1, n_dp)
    ]
    for c in w2_far:
        c.start()

    g_far = []
    mine = None
    for dd in order_dp:
        there = lax.rem(d + dd, n_dp)
        v = gsend[there * n_sp + s].astype(F32)
        for o in range(1, n_sp):
            g_near[dd, o].wait_recv()
            v = v + grecv[there, lax.rem(s + n_sp - o, n_sp)].astype(F32)
        v = v * factor
        if dd == 0:
            mine = v
        else:
            zsend[there] = v.astype(BF16)
            c = remote(zsend.at[there], zrecv.at[d], zs.at[dd - 1], zr.at[dd - 1], at(dd))
            c.start()
            g_far.append(c)

    for c in w2_far:
        c.wait_recv()
    v = w2z[0]
    for o in range(1, n_dp):
        v = v + w2z[o]
    for k in range(9):
        gw2_out[k] = v[4 * k : 4 * k + 4]

    for c in g_far:
        c.wait_recv()
    for dd in range(1, n_dp):
        mine = mine + zrecv[lax.rem(d + dd, n_dp)].astype(F32)
    for ky in range(3):
        for kx in range(3):
            gw1_out[3 * ky + kx] = mine[ky * piece : (ky + 1) * piece, kx * chan : (kx + 1) * chan]

    for c in blocks.values():
        c.wait_send()
    for sides in (feat_halo[0], feat_halo[1], stat_p[1], stat_r[1], noise_edge, pred_edge):
        sides[2]()
    for c in stat_p[0] + stat_r[0] + stat_b + pred_p + pred_r + err_p + err_r + w2_near + w2_far + g_far:
        c.wait_send()
    for c in g_near.values():
        c.wait_send()


def body(
    feat_policy, feat_ref, noise, w1_policy, w1_ref, b1_policy, b1_ref,
    gn_gain_policy, gn_bias_policy, gn_gain_ref, gn_bias_ref,
    w2_policy, w2_ref, time_table, timestep, winner,
):
    _, latents, chan, rows, cols = feat_policy.shape
    out_ch = noise.shape[2]
    n_dp, n_sp, n_t = (lax.axis_size(a) for a in ("dp", "space", "tensor"))
    total, parts = chan * n_t, n_dp * n_sp
    piece = total // parts
    deep = -(-3 * piece // 16) * 16
    dma = pltpu.SemaphoreType.DMA
    near, far = max(n_sp - 1, 1), max(n_t - 1, 1)
    operands = [
        feat_policy.reshape(latents, chan * rows, cols),
        feat_ref.reshape(latents, chan * rows, cols),
        noise.reshape(latents * out_ch, rows, cols),
        w1_policy, w1_ref,
        b1_policy[None], b1_ref[None],
        gn_gain_policy[None], gn_bias_policy[None], gn_gain_ref[None], gn_bias_ref[None],
        w2_policy, w2_ref, time_table.T,
    ]
    scratch = [pltpu.VMEM(a.shape, a.dtype) for a in operands] + [dma((len(operands),))]
    scratch += [
        pltpu.VMEM((2, 2, rows + 2, total, cols), BF16),
        pltpu.VMEM((2, 3 * chan, 3 * total), BF16),
        pltpu.VMEM((2, 2, rows + 2, chan, cols), F32),
        pltpu.VMEM((2, 2, rows, chan, cols), F32),
        pltpu.VMEM((2, 2, rows + 2, chan, cols), BF16),
        pltpu.VMEM((3, n_sp, 8, cols), F32),
        pltpu.VMEM((2, n_t, rows, 8, cols), F32),
        pltpu.VMEM((2, n_t, 8, cols), F32),
        pltpu.VMEM((rows + 2, 8, cols), F32),
        pltpu.VMEM((rows + 2, 8, cols), F32),
        pltpu.VMEM((2, n_sp, 8, cols), F32),
        pltpu.VMEM((3 * chan, latents * rows * cols), BF16),
        pltpu.VMEM((parts, deep, 3 * chan), BF16),
        pltpu.VMEM((n_dp, n_sp, deep, 3 * chan), BF16),
        pltpu.VMEM((n_dp, deep, 3 * chan), BF16),
        pltpu.VMEM((n_dp, deep, 3 * chan), BF16),
        pltpu.VMEM((n_sp, 40, chan), F32),
        pltpu.VMEM((n_dp, 40, chan), F32),
    ]
    for shape in (
        (2, 2, far), (2, 2, n_t), (3, near), (2, 2), (2, far), (2, n_t), (2, near),
        (n_dp, near), (max(n_dp - 1, 1),), (near,), (max(n_dp - 1, 1),), (2,),
    ):
        scratch += [dma(shape), dma(shape)]
    dims = (n_dp, n_sp, n_t, rows, cols, chan, out_ch)
    logit, gw1, gw2 = pl.pallas_call(
        functools.partial(kernel, dims),
        out_shape=[
            jax.ShapeDtypeStruct((1, cols), F32),
            jax.ShapeDtypeStruct((9, piece, chan), F32),
            jax.ShapeDtypeStruct((9, out_ch, chan), F32),
        ],
        in_specs=[pl.BlockSpec(memory_space=pltpu.HBM)] * 14 + [SM] * 2,
        out_specs=[VM] * 3,
        scratch_shapes=scratch,
        compiler_params=pltpu.CompilerParams(
            collective_id=0, has_side_effects=True, vmem_limit_bytes=54500 * 1024
        ),
        name="dpo",
    )(*operands, timestep, winner)
    return logit[0, :1], gw1.transpose(0, 2, 1), gw2


def solution(mesh):
    in_specs = (
        P("dp", None, "tensor", "space", None),
        P("dp", None, "tensor", "space", None),
        P("dp", None, None, "space", None),
        P(None, "tensor", None),
        P(None, "tensor", None),
        P("tensor"),
        P("tensor"),
        P("tensor"),
        P("tensor"),
        P("tensor"),
        P("tensor"),
        P(None, None, "tensor"),
        P(None, None, "tensor"),
        P(None, "tensor"),
        P("dp"),
        P("dp"),
    )
    out_specs = (P("dp"), P(None, "tensor", ("dp", "space")), P(None, None, "tensor"))
    return jax.shard_map(body, mesh=mesh, in_specs=in_specs, out_specs=out_specs, check_vma=False)
```
